32 devices in a mesh: grp: 2 (over x), row: 16 (over z, y, core).
Axes of the slice: x: 2, y: 2, z: 4, core: 2. Of those that a mesh axis runs over, the one named last changes fastest.
Arguments:
- cell_coeffs: float32 [6, 32, 384], P(None, 'row'), may hold values from 0.5 to 2
- z_factor: float32 [4, 64, 384, 128], P(None, ('grp', 'row')), parts along dimension 1, may hold values from -0.022552745 to 0.022552745
- noise_cols: float32 [4, 64, 384, 128], P(None, ('grp', 'row')), parts along dimension 1, may hold values from -0.022552745 to 0.022552745
- q_bar: float32 [4, 64, 384, 256], P(None, ('grp', 'row')), parts along dimension 1, may hold values from -10 to 10
- r_bar: float32 [512, 256], P('grp'), parts along dimension 0, may hold values from -11.085125 to 11.085125
Outputs:
- z_grad: float32 [4, 64, 384, 128], P(None, ('grp', 'row')), parts along dimension 1
- noise_grad: float32 [4, 64, 384, 128], P(None, ('grp', 'row')), parts along dimension 1
The draws below stay inside these ranges and needn't reach their ends.
There are 2 independent parts, one for each index of `grp`. The reference program is written for one: setup_inputs(seed, part) draws one part's arguments, and reference() takes and returns one part's arrays. A program takes and returns all parts, laid end to end along the dimension named above; an argument that names none is the same for every part. Nothing has to cross between parts.
All inputs are finite; a program needn't handle non-finite values.
Results may differ from the reference program's by a relative error of at most 0.000061.
Values sent between devices are 32-bit elements; how exact they have to be, the bound alone decides.
A program may use at most 64 MiB of HBM per device.

```python
import math
import jax
import jax.numpy as jnp
from jax import lax

LX = 384
K = 128
KN = 128
NR = 32
ROWS = 49152


def draw_piece(key, shape):
    return jnp.clip(jax.random.normal(key, shape, jnp.float32), -5.0, 5.0)


def draw_shared(key):
    spread = float(ROWS) ** (-0.5)
    base_z = draw_piece(jax.random.fold_in(key, 11), (4, NR, LX, K))
    base_n = draw_piece(jax.random.fold_in(key, 12), (4, NR, LX, KN))
    loose = draw_piece(jax.random.fold_in(key, 13), (4, NR, LX, K + KN))
    bar_q = jnp.concatenate([base_z, base_n], axis=3) + loose
    bar_r = jnp.clip(jax.random.normal(jax.random.fold_in(key, 14), (K + KN, K + KN), jnp.float32), -5.0, 5.0) * (0.01 * float(ROWS) ** 0.5)
    return (base_z * spread, base_n * spread, bar_q, bar_r)


def draw_z_factor(key, part):
    return draw_shared(key)[0]


def draw_noise_cols(key, part):
    return draw_shared(key)[1]


def draw_q_bar(key, part):
    return draw_shared(key)[2]


def draw_r_bar(key, part):
    return draw_shared(key)[3]


def levels(key, shape, split, least, high):
    loudness = 1.0
    for position, blocks in split:
        draws = jax.random.uniform(jax.random.fold_in(jax.random.fold_in(key, 6), position), (blocks,), jnp.float32, least / len(split), high / len(split))
        loudness = loudness * jnp.repeat(jnp.exp(draws), shape[position] // blocks).reshape((-1,) + (1,) * (len(shape) - 1 - position))
    return loudness


def setup_inputs(seed: int = 0, part: int = 0) -> dict:
    key_of = jax.random.split(jax.random.key(seed), 6)
    part_splits = jax.random.split(jax.random.fold_in(key_of[5], part), 6)
    return {
        "cell_coeffs": jnp.clip(jnp.exp(math.log(2.0) - 1.3862944 * jax.random.uniform(key_of[0], (6, NR, LX), jnp.float32) ** levels(key_of[0], (6, NR, LX), ((1, 16),), -0.2, 0.2)), 0.5, 2.0),
        "z_factor": draw_z_factor(jax.random.fold_in(jax.random.fold_in(key_of[5], part), 71), part),
        "noise_cols": draw_noise_cols(jax.random.fold_in(jax.random.fold_in(key_of[5], part), 71), part),
        "q_bar": draw_q_bar(jax.random.fold_in(jax.random.fold_in(key_of[5], part), 71), part),
        "r_bar": draw_r_bar(jax.random.fold_in(jax.random.fold_in(key_of[5], part), 71), part),
    }


rate_scales = (0.4, 0.4, 0.1, 0.2, 0.1, 0.1)
exact = lax.Precision.HIGHEST

def local_part(values, scaled, transposed):
    detuning = scaled[0][..., None]
    mech_freq = scaled[1][..., None]
    coupling = scaled[2][..., None]
    cavity_loss = scaled[3][..., None]
    phonon_loss = scaled[4][..., None]
    light_x, light_p, motion_x, motion_p = (values[0], values[1], values[2], values[3])
    if transposed:
        return jnp.stack([-0.5 * cavity_loss * light_x + detuning * light_p - 2.0 * coupling * motion_p, -detuning * light_x - 0.5 * cavity_loss * light_p, -2.0 * coupling * light_p - mech_freq * motion_p, mech_freq * motion_x - 0.5 * phonon_loss * motion_p])
    return jnp.stack([-0.5 * cavity_loss * light_x - detuning * light_p, detuning * light_x - 0.5 * cavity_loss * light_p - 2.0 * coupling * motion_x, mech_freq * motion_p, -mech_freq * motion_x - 0.5 * phonon_loss * motion_p - 2.0 * coupling * light_x])

def hop_sources(values, scaled, transposed):
    hopping = scaled[5][..., None]
    if transposed:
        return jnp.stack([hopping * values[0], hopping * values[1]])
    return jnp.stack([values[1], values[0]])

def neighbours(source):
    middle = source[:, 1:-1]
    sideways = jnp.pad(middle, ((0, 0), (0, 0), (1, 1), (0, 0)))
    return source[:, :-2] + source[:, 2:] + sideways[:, :, :-2] + sideways[:, :, 2:]

def hop_add(local_term, hop_sums, scaled, transposed):
    hopping = scaled[5][..., None]
    if transposed:
        return jnp.stack([local_term[0] + hop_sums[1], local_term[1] - hop_sums[0], local_term[2], local_term[3]])
    return jnp.stack([local_term[0] - hopping * hop_sums[0], local_term[1] + hopping * hop_sums[1], local_term[2], local_term[3]])

def apply_full(values, scaled, transposed):
    source = hop_sources(values, scaled, transposed)
    extended = jnp.pad(source, ((0, 0), (1, 1), (0, 0), (0, 0)))
    return hop_add(local_part(values, scaled, transposed), neighbours(extended), scaled, transposed)

def expand(values, scaled, transposed):
    first_term = apply_full(values, scaled, transposed)
    second = apply_full(first_term, scaled, transposed)
    return values + first_term + 0.5 * second

def reference(cell_coeffs, z_factor, noise_cols, q_bar, r_bar):
    scaled = cell_coeffs * jnp.array(rate_scales, jnp.float32)[:, None, None]
    rank_cols = z_factor.shape[3]
    stacked = jnp.concatenate([expand(z_factor, scaled, False), noise_cols], axis=3)
    flat_rows = stacked.reshape(-1, stacked.shape[3])
    bar_rows = q_bar.reshape(-1, q_bar.shape[3])
    gram_matrix = jnp.einsum('ik,il->kl', flat_rows, flat_rows, precision=exact)
    lower_factor = jnp.linalg.cholesky(gram_matrix)
    identity = jnp.eye(gram_matrix.shape[0], dtype=jnp.float32)
    r_inv = lax.linalg.triangular_solve(lower_factor, identity, left_side=True, lower=True).T
    upper_factor = lower_factor.T
    q_fact = jnp.dot(flat_rows, r_inv, precision=exact)
    cross = jnp.einsum('ik,il->kl', bar_rows, q_fact, precision=exact)
    middle = jnp.dot(upper_factor, jnp.triu(r_bar).T, precision=exact) - cross
    symmetric = jnp.tril(middle) + jnp.tril(middle, -1).T
    grad_rows = jnp.dot(bar_rows + jnp.dot(q_fact, symmetric, precision=exact), r_inv.T, precision=exact)
    grad_x = grad_rows.reshape(q_bar.shape)
    z_grad = expand(grad_x[..., :rank_cols], scaled, True)
    return (z_grad, grad_x[..., rank_cols:])
```

```python
import functools

import jax
import jax.numpy as jnp
from jax import lax
from jax.experimental import pallas as pl
from jax.experimental.pallas import tpu as pltpu
from jax.sharding import PartitionSpec as P

rate_scales = (0.4, 0.4, 0.1, 0.2, 0.1, 0.1)
exact = lax.Precision.HIGHEST


def padded(block, sides, width):
    for axis, dim in sides:
        count = lax.axis_size(axis)
        forward = [(i, i + 1) for i in range(count - 1)]
        backward = [(target, source) for source, target in forward]
        low = lax.ppermute(
            lax.slice_in_dim(block, block.shape[dim] - width, None, axis=dim), axis, forward
        )
        high = lax.ppermute(lax.slice_in_dim(block, 0, width, axis=dim), axis, backward)
        block = jnp.concatenate([low, block, high], axis=dim)
    return block


def local_part(values, scaled, transposed):
    detuning = scaled[0][..., None]
    mech_freq = scaled[1][..., None]
    coupling = scaled[2][..., None]
    cavity_loss = scaled[3][..., None]
    phonon_loss = scaled[4][..., None]
    light_x, light_p, motion_x, motion_p = (values[0], values[1], values[2], values[3])
    if transposed:
        return jnp.stack(
            [
                -0.5 * cavity_loss * light_x + detuning * light_p - 2.0 * coupling * motion_p,
                -detuning * light_x - 0.5 * cavity_loss * light_p,
                -2.0 * coupling * light_p - mech_freq * motion_p,
                mech_freq * motion_x - 0.5 * phonon_loss * motion_p,
            ]
        )
    return jnp.stack(
        [
            -0.5 * cavity_loss * light_x - detuning * light_p,
            detuning * light_x - 0.5 * cavity_loss * light_p - 2.0 * coupling * motion_x,
            mech_freq * motion_p,
            -mech_freq * motion_x - 0.5 * phonon_loss * motion_p - 2.0 * coupling * light_x,
        ]
    )


def hop_sources(values, scaled, transposed):
    hopping = scaled[5][..., None]
    if transposed:
        return jnp.stack([hopping * values[0], hopping * values[1]])
    return jnp.stack([values[1], values[0]])


def neighbours(source):
    middle = source[:, 1:-1]
    sideways = jnp.pad(middle, ((0, 0), (0, 0), (1, 1), (0, 0)))
    return source[:, :-2] + source[:, 2:] + sideways[:, :, :-2] + sideways[:, :, 2:]


def hop_add(local_term, hop_sums, scaled, transposed):
    hopping = scaled[5][..., None]
    if transposed:
        return jnp.stack(
            [local_term[0] + hop_sums[1], local_term[1] - hop_sums[0], local_term[2], local_term[3]]
        )
    return jnp.stack(
        [
            local_term[0] - hopping * hop_sums[0],
            local_term[1] + hopping * hop_sums[1],
            local_term[2],
            local_term[3],
        ]
    )


def rim_apply(values, scaled, transposed):
    source = hop_sources(values, scaled, transposed)
    extended = padded(source, (("row", 1),), 1)
    return hop_add(local_part(values, scaled, transposed), neighbours(extended), scaled, transposed)


def shallow_expand(values, scaled, transposed):
    first_term = rim_apply(values, scaled, transposed)
    second = rim_apply(first_term, scaled, transposed)
    return values + first_term + 0.5 * second


def sum_kernel(count, part_ref, out_ref, half_in, half_sum, quarter_in, quarter_sum, piece_in, full, send_sem, recv_sem, peer_send, peer_recv, back_send, back_recv):
    rows = part_ref.shape[0]
    peers = count // 4
    half, quarter, piece = rows // 2, rows // 4, rows // count
    me = lax.axis_index("row")
    low, mid, top = lax.rem(me, 2), lax.rem(me // 2, 2), me // 4
    pair = me + 1 - 2 * low
    across = me + 2 - 4 * mid

    def other(step):
        return lax.rem(top + step, peers)

    def device(step):
        return {"row": other(step) * 4 + lax.rem(me, 4)}

    barrier = pltpu.get_barrier_semaphore()
    pl.semaphore_signal(barrier, inc=1, device_id={"row": pair}, device_id_type=pl.DeviceIdType.MESH)
    pl.semaphore_signal(barrier, inc=1, device_id={"row": across}, device_id_type=pl.DeviceIdType.MESH)
    for step in range(1, peers):
        pl.semaphore_signal(barrier, inc=1, device_id=device(step), device_id_type=pl.DeviceIdType.MESH)
    pl.semaphore_wait(barrier, peers + 1)

    def swap(source, target, slot, where):
        return pltpu.make_async_remote_copy(
            src_ref=source,
            dst_ref=target,
            send_sem=send_sem.at[slot],
            recv_sem=recv_sem.at[slot],
            device_id={"row": where},
            device_id_type=pl.DeviceIdType.MESH,
        )

    first = swap(part_ref.at[pl.ds(pl.multiple_of((1 - low) * half, 8), half)], half_in, 0, pair)
    first.start()
    first.wait()
    half_sum[...] = part_ref[pl.ds(pl.multiple_of(low * half, 8), half)] + half_in[...]
    second = swap(half_sum.at[pl.ds(pl.multiple_of((1 - mid) * quarter, 8), quarter)], quarter_in, 1, across)
    second.start()
    second.wait()
    quarter_sum[...] = half_sum[pl.ds(pl.multiple_of(mid * quarter, 8), quarter)] + quarter_in[...]

    outgoing = []
    for step in range(1, peers):
        copy = pltpu.make_async_remote_copy(
            src_ref=quarter_sum.at[pl.ds(pl.multiple_of(other(step) * piece, 8), piece)],
            dst_ref=piece_in.at[step],
            send_sem=peer_send.at[step],
            recv_sem=peer_recv.at[step],
            device_id=device(step),
            device_id_type=pl.DeviceIdType.MESH,
        )
        copy.start()
        outgoing.append(copy)
    total = quarter_sum[pl.ds(pl.multiple_of(top * piece, 8), piece)]
    for step, copy in enumerate(outgoing, 1):
        copy.wait()
        total = total + piece_in[step]
    base = low * half + mid * quarter
    mine = pl.ds(pl.multiple_of(base + top * piece, 8), piece)
    full[mine] = total
    returning = []
    for step in range(1, peers):
        copy = pltpu.make_async_remote_copy(
            src_ref=full.at[mine],
            dst_ref=full.at[mine],
            send_sem=back_send.at[step],
            recv_sem=back_recv.at[step],
            device_id=device(step),
            device_id_type=pl.DeviceIdType.MESH,
        )
        copy.start()
        returning.append(copy)
    for copy in returning:
        copy.wait()
    own_quarter = full.at[pl.ds(pl.multiple_of(base, 8), quarter)]
    third = swap(own_quarter, own_quarter, 2, across)
    third.start()
    third.wait()
    own_half = full.at[pl.ds(pl.multiple_of(low * half, 8), half)]
    fourth = swap(own_half, own_half, 3, pair)
    fourth.start()
    fourth.wait()
    out_ref[...] = full[...]


def device_sum(part):
    count = lax.axis_size("row")
    rows, cols = part.shape
    peers = count // 4
    return pl.pallas_call(
        functools.partial(sum_kernel, count),
        out_shape=jax.ShapeDtypeStruct(part.shape, jnp.float32),
        in_specs=[pl.BlockSpec(memory_space=pltpu.VMEM)],
        out_specs=pl.BlockSpec(memory_space=pltpu.VMEM),
        scratch_shapes=[
            pltpu.VMEM((rows // 2, cols), jnp.float32),
            pltpu.VMEM((rows // 2, cols), jnp.float32),
            pltpu.VMEM((rows // 4, cols), jnp.float32),
            pltpu.VMEM((rows // 4, cols), jnp.float32),
            pltpu.VMEM((peers, rows // count, cols), jnp.float32),
            pltpu.VMEM((rows, cols), jnp.float32),
            pltpu.SemaphoreType.DMA((4,)),
            pltpu.SemaphoreType.DMA((4,)),
            pltpu.SemaphoreType.DMA((peers,)),
            pltpu.SemaphoreType.DMA((peers,)),
            pltpu.SemaphoreType.DMA((peers,)),
            pltpu.SemaphoreType.DMA((peers,)),
        ],
        compiler_params=pltpu.CompilerParams(collective_id=0, has_side_effects=True, vmem_limit_bytes=24 * 2**20),
    )(part)


tile = 32


def tile_inverse(block):
    shape = (tile, tile)
    row_ids = lax.broadcasted_iota(jnp.int32, shape, 0)
    col_ids = lax.broadcasted_iota(jnp.int32, shape, 1)
    right = (row_ids == col_ids).astype(jnp.float32)
    left = block
    scale = jnp.zeros(shape, jnp.float32)
    for start in range(0, tile, 8):
        columns = [
            jnp.broadcast_to(left[start:, start + k : start + k + 1], (tile - start, tile)) for k in range(8)
        ]
        below_left, below_right = left[start:], right[start:]
        ids = row_ids[start:]
        for j in range(8):
            pivot = columns[j][j : j + 1]
            factor = jnp.where(ids > start + j, columns[j] * (1.0 / pivot), 0.0)
            scale = jnp.where(row_ids == start + j, lax.rsqrt(pivot), scale)
            for k in range(j + 1, 8):
                columns[k] = columns[k] - factor * columns[k][j : j + 1]
            below_left = below_left - factor * below_left[j : j + 1]
            below_right = below_right - factor * below_right[j : j + 1]
        if start:
            left = jnp.concatenate([left[:start], below_left], axis=0)
            right = jnp.concatenate([right[:start], below_right], axis=0)
        else:
            left, right = below_left, below_right
    return right * scale


def mul(a, b, contract):
    return lax.dot_general(a, b, ((contract[0:1], contract[1:2]), ((), ())), precision=exact, preferred_element_type=jnp.float32)


def factor_kernel(gram_ref, cross_ref, bar_ref, inv_ref, mix_ref, work):
    size = gram_ref.shape[0]
    row_ids = lax.broadcasted_iota(jnp.int32, (size, size), 0)
    col_ids = lax.broadcasted_iota(jnp.int32, (size, size), 1)
    work[:, :size] = gram_ref[...]
    work[:, size:] = (row_ids == col_ids).astype(jnp.float32)
    for start in range(0, size, tile):
        stop = start + tile
        small = tile_inverse(work[start:stop, start:stop])
        panel = mul(small, work[start:stop, :], (1, 0))
        work[start:stop, :] = panel
        if stop < size:
            update = mul(panel[:, :size].T, panel, (1, 0))
            work[stop:, :] = work[stop:, :] - update[stop:]
    upper = jnp.where(row_ids <= col_ids, work[:, :size], 0.0)
    inverse = jnp.where(row_ids >= col_ids, work[:, size:], 0.0)
    inv_ref[...] = inverse
    bar = jnp.where(row_ids <= col_ids, bar_ref[...], 0.0)
    middle = mul(upper, bar, (1, 1)) - mul(cross_ref[...], inverse, (1, 1))
    symmetric = jnp.where(row_ids >= col_ids, middle, middle.T)
    mix_ref[...] = mul(inverse.T, mul(symmetric, inverse, (1, 0)), (1, 0))


def factor(gram, cross, r_bar):
    size = gram.shape[0]
    shape = jax.ShapeDtypeStruct((size, size), jnp.float32)
    whole = pl.BlockSpec(memory_space=pltpu.VMEM)
    return pl.pallas_call(
        factor_kernel,
        out_shape=(shape, shape),
        in_specs=[whole] * 3,
        out_specs=(whole, whole),
        scratch_shapes=[pltpu.VMEM((size, 2 * size), jnp.float32)],
        compiler_params=pltpu.CompilerParams(vmem_limit_bytes=24 * 2**20),
    )(gram, cross, r_bar)


def on_device(cell_coeffs, z_factor, noise_cols, q_bar, r_bar):
    scaled = cell_coeffs * jnp.array(rate_scales, jnp.float32)[:, None, None]
    rank_cols = z_factor.shape[3]

    def expand(values, transposed):
        return shallow_expand(values, scaled, transposed)

    stacked = jnp.concatenate([expand(z_factor, False), noise_cols], axis=3)
    flat_rows = stacked.reshape(-1, stacked.shape[3])
    bar_rows = q_bar.reshape(-1, q_bar.shape[3])
    both = jnp.concatenate([flat_rows, bar_rows], axis=1)
    products = lax.dot_general(both, flat_rows, (((0,), (0,)), ((), ())), precision=lax.Precision.HIGH)
    products = device_sum(products)
    size = flat_rows.shape[1]
    inverse, mix = factor(products[:size], products[size:], r_bar)
    grad_rows = jnp.dot(bar_rows, inverse, precision=lax.Precision.HIGH) + jnp.dot(flat_rows, mix, precision=lax.Precision.HIGH)
    grad_x = grad_rows.reshape(q_bar.shape)
    z_grad = expand(grad_x[..., :rank_cols], True)
    return (z_grad, grad_x[..., rank_cols:])


def solution(mesh):
    return jax.shard_map(
        on_device,
        mesh=mesh,
        in_specs=(
            P(None, "row", None),
            P(None, ("grp", "row"), None, None),
            P(None, ("grp", "row"), None, None),
            P(None, ("grp", "row"), None, None),
            P("grp", None),
        ),
        out_specs=(P(None, ("grp", "row"), None, None), P(None, ("grp", "row"), None, None)),
        check_vma=False,
    )
```

```python
import functools

import jax
import jax.numpy as jnp
from jax import lax
from jax.experimental import pallas as pl
from jax.experimental.pallas import tpu as pltpu
from jax.sharding import PartitionSpec as P

rate_scales = (0.4, 0.4, 0.1, 0.2, 0.1, 0.1)
exact = lax.Precision.HIGHEST


parts = 4
margin = 8


def step_kernel(count, transposed, coef_ref, value_ref, out_ref, coefs, first, source, source_two, send_low, recv_low, send_high, recv_high):
    rows, cells, cols = value_ref.shape[1:]
    chunk = cells // parts
    me = lax.axis_index("row")
    has_low, has_high = me > 0, me < count - 1

    def link(buffer, stage, piece, upward):
        cut = pl.ds(margin + piece * chunk, chunk)
        sends, recvs = (send_high, recv_high) if upward else (send_low, recv_low)
        slot = stage * parts + piece
        return pltpu.make_async_remote_copy(
            src_ref=buffer.at[:, rows if upward else 1, cut],
            dst_ref=buffer.at[:, 0 if upward else rows + 1, cut],
            send_sem=sends.at[slot],
            recv_sem=recvs.at[slot],
            device_id={"row": me + 1 if upward else me - 1},
            device_id_type=pl.DeviceIdType.MESH,
        )

    def send(buffer, stage, piece):
        @pl.when(has_high)
        def _():
            link(buffer, stage, piece, True).start()

        @pl.when(has_low)
        def _():
            link(buffer, stage, piece, False).start()

    def receive(buffer, stage, piece):
        @pl.when(has_low)
        def _():
            link(buffer, stage, piece, True).wait_recv()

        @pl.when(has_high)
        def _():
            link(buffer, stage, piece, False).wait_recv()

    barrier = pltpu.get_barrier_semaphore()

    @pl.when(has_low)
    def _():
        pl.semaphore_signal(barrier, inc=1, device_id={"row": me - 1}, device_id_type=pl.DeviceIdType.MESH)

    @pl.when(has_high)
    def _():
        pl.semaphore_signal(barrier, inc=1, device_id={"row": me + 1}, device_id_type=pl.DeviceIdType.MESH)

    def coef(kind, row, piece):
        return coefs[kind * rows + row, piece * chunk : (piece + 1) * chunk]

    def at(piece):
        return slice(piece * chunk, (piece + 1) * chunk)

    def inner(piece, shift=0):
        return slice(margin + piece * chunk + shift, margin + (piece + 1) * chunk + shift)

    def spread(kind):
        for row in range(rows):
            index = kind * rows + row
            coefs[index] = jnp.broadcast_to(coef_ref[:, index : index + 1], (cells, cols))

    def fill(buffer, values, piece):
        for row in range(rows):
            for quad in range(2):
                value = values[quad, row, at(piece)]
                if transposed:
                    value = value * coef(5, row, piece)
                buffer[quad, row + 1, inner(piece)] = value

    def zero_rim(buffer):
        for quad in range(2):
            for row in range(rows):
                buffer[quad, row + 1, :margin] = jnp.zeros((margin, cols), jnp.float32)
                buffer[quad, row + 1, margin + cells :] = jnp.zeros((margin, cols), jnp.float32)

        @pl.when(jnp.logical_not(has_low))
        def _():
            buffer[:, 0] = jnp.zeros(buffer.shape[:1] + buffer.shape[2:], jnp.float32)

        @pl.when(jnp.logical_not(has_high))
        def _():
            buffer[:, rows + 1] = jnp.zeros(buffer.shape[:1] + buffer.shape[2:], jnp.float32)

    def local(values, buffer, row, piece):
        xa, pa, xb, pb = [values[quad, row, at(piece)] for quad in range(4)]
        detuning, mech, coupling, cavity, phonon, hopping = [coef(kind, row, piece) for kind in range(6)]
        sums = []
        for quad in range(2):
            total = buffer[quad, row + 1, inner(piece, -1)] + buffer[quad, row + 1, inner(piece, 1)]
            if row > 0:
                total = total + buffer[quad, row, inner(piece)]
            if row < rows - 1:
                total = total + buffer[quad, row + 2, inner(piece)]
            sums.append(total)
        if transposed:
            return (
                -0.5 * cavity * xa + detuning * pa - 2.0 * coupling * pb + sums[1],
                -detuning * xa - 0.5 * cavity * pa - sums[0],
                -2.0 * coupling * pa - mech * pb,
                mech * xb - 0.5 * phonon * pb,
            )
        return (
            -0.5 * cavity * xa - detuning * pa - hopping * sums[1],
            detuning * xa - 0.5 * cavity * pa - 2.0 * coupling * xb + hopping * sums[0],
            mech * pb,
            -mech * xb - 0.5 * phonon * pb - 2.0 * coupling * xa,
        )

    def edges(buffer, piece):
        found = []
        for row, halo in ((0, 0), (rows - 1, rows + 1)):
            light_x, light_p = buffer[0, halo, inner(piece)], buffer[1, halo, inner(piece)]
            if transposed:
                found.append((row, light_p, -light_x))
            else:
                hopping = coef(5, row, piece)
                found.append((row, -hopping * light_p, hopping * light_x))
        return found

    spread(5)
    fill(source, value_ref, 0)

    pl.semaphore_wait(barrier, jnp.where(me > 0, 1, 0) + jnp.where(me < count - 1, 1, 0))

    send(source, 0, 0)
    for piece in range(1, parts):
        fill(source, value_ref, piece)
        send(source, 0, piece)
    zero_rim(source)
    zero_rim(source_two)
    for kind in range(5):
        spread(kind)
    for piece in range(parts):
        for row in range(rows):
            for quad, value in enumerate(local(value_ref, source, row, piece)):
                first[quad, row, at(piece)] = value
    for piece in range(parts):
        receive(source, 0, piece)
        for row, add_x, add_p in edges(source, piece):
            first[0, row, at(piece)] = first[0, row, at(piece)] + add_x
            first[1, row, at(piece)] = first[1, row, at(piece)] + add_p
        fill(source_two, first, piece)
        send(source_two, 1, piece)
    for piece in range(parts):
        for row in range(rows):
            for quad, value in enumerate(local(first, source_two, row, piece)):
                out_ref[quad, row, at(piece)] = (
                    value_ref[quad, row, at(piece)] + first[quad, row, at(piece)] + 0.5 * value
                )
    for piece in range(parts):
        receive(source_two, 1, piece)
        for row, add_x, add_p in edges(source_two, piece):
            out_ref[0, row, at(piece)] = out_ref[0, row, at(piece)] + 0.5 * add_x
            out_ref[1, row, at(piece)] = out_ref[1, row, at(piece)] + 0.5 * add_p
    for stage, buffer in enumerate((source, source_two)):
        for piece in range(parts):

            @pl.when(has_high)
            def _():
                link(buffer, stage, piece, True).wait_send()

            @pl.when(has_low)
            def _():
                link(buffer, stage, piece, False).wait_send()


def second_order(coef_columns, values, transposed):
    count = lax.axis_size("row")
    quads, rows, cells, cols = values.shape
    whole = pl.BlockSpec(memory_space=pltpu.VMEM)
    return pl.pallas_call(
        functools.partial(step_kernel, count, transposed),
        out_shape=jax.ShapeDtypeStruct(values.shape, jnp.float32),
        in_specs=[whole] * 2,
        out_specs=whole,
        scratch_shapes=[
            pltpu.VMEM((coef_columns.shape[1], cells, cols), jnp.float32),
            pltpu.VMEM((quads, rows, cells, cols), jnp.float32),
            pltpu.VMEM((2, rows + 2, cells + 2 * margin, cols), jnp.float32),
            pltpu.VMEM((2, rows + 2, cells + 2 * margin, cols), jnp.float32),
        ]
        + [pltpu.SemaphoreType.DMA((2 * parts,))] * 4,
        compiler_params=pltpu.CompilerParams(
            collective_id=2 if transposed else 1, has_side_effects=True, vmem_limit_bytes=40 * 2**20
        ),
    )(coef_columns, values)


def sum_kernel(count, part_ref, out_ref, half_in, half_sum, quarter_in, quarter_sum, piece_in, full, send_sem, recv_sem, peer_send, peer_recv, back_send, back_recv):
    rows = part_ref.shape[0]
    peers = count // 4
    half, quarter, piece = rows // 2, rows // 4, rows // count
    me = lax.axis_index("row")
    low, mid, top = lax.rem(me, 2), lax.rem(me // 2, 2), me // 4
    pair = me + 1 - 2 * low
    across = me + 2 - 4 * mid

    def other(step):
        return lax.rem(top + step, peers)

    def device(step):
        return {"row": other(step) * 4 + lax.rem(me, 4)}

    barrier = pltpu.get_barrier_semaphore()
    pl.semaphore_signal(barrier, inc=1, device_id={"row": pair}, device_id_type=pl.DeviceIdType.MESH)
    pl.semaphore_signal(barrier, inc=1, device_id={"row": across}, device_id_type=pl.DeviceIdType.MESH)
    for step in range(1, peers):
        pl.semaphore_signal(barrier, inc=1, device_id=device(step), device_id_type=pl.DeviceIdType.MESH)
    pl.semaphore_wait(barrier, peers + 1)

    def swap(source, target, slot, where):
        return pltpu.make_async_remote_copy(
            src_ref=source,
            dst_ref=target,
            send_sem=send_sem.at[slot],
            recv_sem=recv_sem.at[slot],
            device_id={"row": where},
            device_id_type=pl.DeviceIdType.MESH,
        )

    first = swap(part_ref.at[pl.ds(pl.multiple_of((1 - low) * half, 8), half)], half_in, 0, pair)
    first.start()
    first.wait()
    half_sum[...] = part_ref[pl.ds(pl.multiple_of(low * half, 8), half)] + half_in[...]
    second = swap(half_sum.at[pl.ds(pl.multiple_of((1 - mid) * quarter, 8), quarter)], quarter_in, 1, across)
    second.start()
    second.wait()
    quarter_sum[...] = half_sum[pl.ds(pl.multiple_of(mid * quarter, 8), quarter)] + quarter_in[...]

    outgoing = []
    for step in range(1, peers):
        copy = pltpu.make_async_remote_copy(
            src_ref=quarter_sum.at[pl.ds(pl.multiple_of(other(step) * piece, 8), piece)],
            dst_ref=piece_in.at[step],
            send_sem=peer_send.at[step],
            recv_sem=peer_recv.at[step],
            device_id=device(step),
            device_id_type=pl.DeviceIdType.MESH,
        )
        copy.start()
        outgoing.append(copy)
    total = quarter_sum[pl.ds(pl.multiple_of(top * piece, 8), piece)]
    for step, copy in enumerate(outgoing, 1):
        copy.wait()
        total = total + piece_in[step]
    base = low * half + mid * quarter
    mine = pl.ds(pl.multiple_of(base + top * piece, 8), piece)
    full[mine] = total
    returning = []
    for step in range(1, peers):
        copy = pltpu.make_async_remote_copy(
            src_ref=full.at[mine],
            dst_ref=full.at[mine],
            send_sem=back_send.at[step],
            recv_sem=back_recv.at[step],
            device_id=device(step),
            device_id_type=pl.DeviceIdType.MESH,
        )
        copy.start()
        returning.append(copy)
    for copy in returning:
        copy.wait()
    own_quarter = full.at[pl.ds(pl.multiple_of(base, 8), quarter)]
    third = swap(own_quarter, own_quarter, 2, across)
    third.start()
    third.wait()
    own_half = full.at[pl.ds(pl.multiple_of(low * half, 8), half)]
    fourth = swap(own_half, own_half, 3, pair)
    fourth.start()
    fourth.wait()
    out_ref[...] = full[...]


def device_sum(part):
    count = lax.axis_size("row")
    rows, cols = part.shape
    peers = count // 4
    return pl.pallas_call(
        functools.partial(sum_kernel, count),
        out_shape=jax.ShapeDtypeStruct(part.shape, jnp.float32),
        in_specs=[pl.BlockSpec(memory_space=pltpu.VMEM)],
        out_specs=pl.BlockSpec(memory_space=pltpu.VMEM),
        scratch_shapes=[
            pltpu.VMEM((rows // 2, cols), jnp.float32),
            pltpu.VMEM((rows // 2, cols), jnp.float32),
            pltpu.VMEM((rows // 4, cols), jnp.float32),
            pltpu.VMEM((rows // 4, cols), jnp.float32),
            pltpu.VMEM((peers, rows // count, cols), jnp.float32),
            pltpu.VMEM((rows, cols), jnp.float32),
            pltpu.SemaphoreType.DMA((4,)),
            pltpu.SemaphoreType.DMA((4,)),
            pltpu.SemaphoreType.DMA((peers,)),
            pltpu.SemaphoreType.DMA((peers,)),
            pltpu.SemaphoreType.DMA((peers,)),
            pltpu.SemaphoreType.DMA((peers,)),
        ],
        compiler_params=pltpu.CompilerParams(collective_id=0, has_side_effects=True, vmem_limit_bytes=24 * 2**20),
    )(part)


tile = 32


def tile_inverse(block):
    shape = (tile, tile)
    row_ids = lax.broadcasted_iota(jnp.int32, shape, 0)
    col_ids = lax.broadcasted_iota(jnp.int32, shape, 1)
    right = (row_ids == col_ids).astype(jnp.float32)
    left = block
    scale = jnp.zeros(shape, jnp.float32)
    for start in range(0, tile, 8):
        columns = [
            jnp.broadcast_to(left[start:, start + k : start + k + 1], (tile - start, tile)) for k in range(8)
        ]
        below_left, below_right = left[start:], right[start:]
        ids = row_ids[start:]
        for j in range(8):
            pivot = columns[j][j : j + 1]
            factor = jnp.where(ids > start + j, columns[j] * (1.0 / pivot), 0.0)
            scale = jnp.where(row_ids == start + j, lax.rsqrt(pivot), scale)
            for k in range(j + 1, 8):
                columns[k] = columns[k] - factor * columns[k][j : j + 1]
            below_left = below_left - factor * below_left[j : j + 1]
            below_right = below_right - factor * below_right[j : j + 1]
        if start:
            left = jnp.concatenate([left[:start], below_left], axis=0)
            right = jnp.concatenate([right[:start], below_right], axis=0)
        else:
            left, right = below_left, below_right
    return right * scale


def mul(a, b, contract):
    return lax.dot_general(a, b, ((contract[0:1], contract[1:2]), ((), ())), precision=exact, preferred_element_type=jnp.float32)


def factor_kernel(gram_ref, cross_ref, bar_ref, inv_ref, mix_ref, work):
    size = gram_ref.shape[0]
    row_ids = lax.broadcasted_iota(jnp.int32, (size, size), 0)
    col_ids = lax.broadcasted_iota(jnp.int32, (size, size), 1)
    work[:, :size] = gram_ref[...]
    work[:, size:] = (row_ids == col_ids).astype(jnp.float32)
    for start in range(0, size, tile):
        stop = start + tile
        small = tile_inverse(work[start:stop, start:stop])
        panel = mul(small, work[start:stop, :], (1, 0))
        work[start:stop, :] = panel
        if stop < size:
            update = mul(panel[:, :size].T, panel, (1, 0))
            work[stop:, :] = work[stop:, :] - update[stop:]
    upper = jnp.where(row_ids <= col_ids, work[:, :size], 0.0)
    inverse = jnp.where(row_ids >= col_ids, work[:, size:], 0.0)
    inv_ref[...] = inverse
    bar = jnp.where(row_ids <= col_ids, bar_ref[...], 0.0)
    middle = mul(upper, bar, (1, 1)) - mul(cross_ref[...], inverse, (1, 1))
    symmetric = jnp.where(row_ids >= col_ids, middle, middle.T)
    mix_ref[...] = mul(inverse.T, mul(symmetric, inverse, (1, 0)), (1, 0))


def factor(gram, cross, r_bar):
    size = gram.shape[0]
    shape = jax.ShapeDtypeStruct((size, size), jnp.float32)
    whole = pl.BlockSpec(memory_space=pltpu.VMEM)
    return pl.pallas_call(
        factor_kernel,
        out_shape=(shape, shape),
        in_specs=[whole] * 3,
        out_specs=(whole, whole),
        scratch_shapes=[pltpu.VMEM((size, 2 * size), jnp.float32)],
        compiler_params=pltpu.CompilerParams(vmem_limit_bytes=24 * 2**20),
    )(gram, cross, r_bar)


def on_device(cell_coeffs, z_factor, noise_cols, q_bar, r_bar):
    scaled = cell_coeffs * jnp.array(rate_scales, jnp.float32)[:, None, None]
    rank_cols = z_factor.shape[3]
    coef_columns = scaled.reshape(-1, scaled.shape[2]).T

    stacked = jnp.concatenate([second_order(coef_columns, z_factor, False), noise_cols], axis=3)
    flat_rows = stacked.reshape(-1, stacked.shape[3])
    bar_rows = q_bar.reshape(-1, q_bar.shape[3])
    both = jnp.concatenate([flat_rows, bar_rows], axis=1)
    products = lax.dot_general(both, flat_rows, (((0,), (0,)), ((), ())), precision=lax.Precision.HIGH)
    products = device_sum(products)
    size = flat_rows.shape[1]
    inverse, mix = factor(products[:size], products[size:], r_bar)
    grad_rows = jnp.dot(bar_rows, inverse, precision=lax.Precision.HIGH) + jnp.dot(flat_rows, mix, precision=lax.Precision.HIGH)
    grad_x = grad_rows.reshape(q_bar.shape)
    z_grad = second_order(coef_columns, grad_x[..., :rank_cols], True)
    return (z_grad, grad_x[..., rank_cols:])


def solution(mesh):
    return jax.shard_map(
        on_device,
        mesh=mesh,
        in_specs=(
            P(None, "row", None),
            P(None, ("grp", "row"), None, None),
            P(None, ("grp", "row"), None, None),
            P(None, ("grp", "row"), None, None),
            P("grp", None),
        ),
        out_specs=(P(None, ("grp", "row"), None, None), P(None, ("grp", "row"), None, None)),
        check_vma=False,
    )
```

```python
import functools

import jax
import jax.numpy as jnp
from jax import lax
from jax.experimental import pallas as pl
from jax.experimental.pallas import tpu as pltpu
from jax.sharding import PartitionSpec as P

rate_scales = (0.4, 0.4, 0.1, 0.2, 0.1, 0.1)
exact = lax.Precision.HIGHEST


parts = 4
margin = 8


def step_kernel(count, transposed, coef_ref, value_ref, out_ref, coefs, first, source, source_two, send_low, recv_low, send_high, recv_high):
    rows, cells, cols = value_ref.shape[1:]
    chunk = cells // parts
    me = lax.axis_index("row")
    has_low, has_high = me > 0, me < count - 1

    def link(buffer, stage, piece, upward):
        cut = pl.ds(margin + piece * chunk, chunk)
        sends, recvs = (send_high, recv_high) if upward else (send_low, recv_low)
        slot = stage * parts + piece
        return pltpu.make_async_remote_copy(
            src_ref=buffer.at[:, rows if upward else 1, cut],
            dst_ref=buffer.at[:, 0 if upward else rows + 1, cut],
            send_sem=sends.at[slot],
            recv_sem=recvs.at[slot],
            device_id={"row": me + 1 if upward else me - 1},
            device_id_type=pl.DeviceIdType.MESH,
        )

    def send(buffer, stage, piece):
        @pl.when(has_high)
        def _():
            link(buffer, stage, piece, True).start()

        @pl.when(has_low)
        def _():
            link(buffer, stage, piece, False).start()

    def receive(buffer, stage, piece):
        @pl.when(has_low)
        def _():
            link(buffer, stage, piece, True).wait_recv()

        @pl.when(has_high)
        def _():
            link(buffer, stage, piece, False).wait_recv()

    barrier = pltpu.get_barrier_semaphore()

    @pl.when(has_low)
    def _():
        pl.semaphore_signal(barrier, inc=1, device_id={"row": me - 1}, device_id_type=pl.DeviceIdType.MESH)

    @pl.when(has_high)
    def _():
        pl.semaphore_signal(barrier, inc=1, device_id={"row": me + 1}, device_id_type=pl.DeviceIdType.MESH)

    def coef(kind, row, piece):
        return coefs[kind * rows + row, piece * chunk : (piece + 1) * chunk]

    def at(piece):
        return slice(piece * chunk, (piece + 1) * chunk)

    def inner(piece, shift=0):
        return slice(margin + piece * chunk + shift, margin + (piece + 1) * chunk + shift)

    def spread(kind):
        for row in range(rows):
            index = kind * rows + row
            coefs[index] = jnp.broadcast_to(coef_ref[:, index : index + 1], (cells, cols))

    def fill(buffer, values, piece):
        for row in range(rows):
            for quad in range(2):
                value = values[quad, row, at(piece)]
                if transposed:
                    value = value * coef(5, row, piece)
                buffer[quad, row + 1, inner(piece)] = value

    def zero_rim(buffer):
        for quad in range(2):
            for row in range(rows):
                buffer[quad, row + 1, :margin] = jnp.zeros((margin, cols), jnp.float32)
                buffer[quad, row + 1, margin + cells :] = jnp.zeros((margin, cols), jnp.float32)

        @pl.when(jnp.logical_not(has_low))
        def _():
            buffer[:, 0] = jnp.zeros(buffer.shape[:1] + buffer.shape[2:], jnp.float32)

        @pl.when(jnp.logical_not(has_high))
        def _():
            buffer[:, rows + 1] = jnp.zeros(buffer.shape[:1] + buffer.shape[2:], jnp.float32)

    def local(values, buffer, row, piece):
        xa, pa, xb, pb = [values[quad, row, at(piece)] for quad in range(4)]
        detuning, mech, coupling, cavity, phonon, hopping = [coef(kind, row, piece) for kind in range(6)]
        sums = []
        for quad in range(2):
            total = buffer[quad, row + 1, inner(piece, -1)] + buffer[quad, row + 1, inner(piece, 1)]
            if row > 0:
                total = total + buffer[quad, row, inner(piece)]
            if row < rows - 1:
                total = total + buffer[quad, row + 2, inner(piece)]
            sums.append(total)
        if transposed:
            return (
                -0.5 * cavity * xa + detuning * pa - 2.0 * coupling * pb + sums[1],
                -detuning * xa - 0.5 * cavity * pa - sums[0],
                -2.0 * coupling * pa - mech * pb,
                mech * xb - 0.5 * phonon * pb,
            )
        return (
            -0.5 * cavity * xa - detuning * pa - hopping * sums[1],
            detuning * xa - 0.5 * cavity * pa - 2.0 * coupling * xb + hopping * sums[0],
            mech * pb,
            -mech * xb - 0.5 * phonon * pb - 2.0 * coupling * xa,
        )

    def edges(buffer, piece):
        found = []
        for row, halo in ((0, 0), (rows - 1, rows + 1)):
            light_x, light_p = buffer[0, halo, inner(piece)], buffer[1, halo, inner(piece)]
            if transposed:
                found.append((row, light_p, -light_x))
            else:
                hopping = coef(5, row, piece)
                found.append((row, -hopping * light_p, hopping * light_x))
        return found

    spread(5)
    fill(source, value_ref, 0)

    pl.semaphore_wait(barrier, jnp.where(me > 0, 1, 0) + jnp.where(me < count - 1, 1, 0))

    send(source, 0, 0)
    for piece in range(1, parts):
        fill(source, value_ref, piece)
        send(source, 0, piece)
    zero_rim(source)
    zero_rim(source_two)
    for kind in range(5):
        spread(kind)
    for piece in range(parts):
        for row in range(rows):
            for quad, value in enumerate(local(value_ref, source, row, piece)):
                first[quad, row, at(piece)] = value
    for piece in range(parts):
        receive(source, 0, piece)
        for row, add_x, add_p in edges(source, piece):
            first[0, row, at(piece)] = first[0, row, at(piece)] + add_x
            first[1, row, at(piece)] = first[1, row, at(piece)] + add_p
        fill(source_two, first, piece)
        send(source_two, 1, piece)
    for piece in range(parts):
        for row in range(rows):
            for quad, value in enumerate(local(first, source_two, row, piece)):
                out_ref[quad, row, at(piece)] = (
                    value_ref[quad, row, at(piece)] + first[quad, row, at(piece)] + 0.5 * value
                )
    for piece in range(parts):
        receive(source_two, 1, piece)
        for row, add_x, add_p in edges(source_two, piece):
            out_ref[0, row, at(piece)] = out_ref[0, row, at(piece)] + 0.5 * add_x
            out_ref[1, row, at(piece)] = out_ref[1, row, at(piece)] + 0.5 * add_p
    for stage, buffer in enumerate((source, source_two)):
        for piece in range(parts):

            @pl.when(has_high)
            def _():
                link(buffer, stage, piece, True).wait_send()

            @pl.when(has_low)
            def _():
                link(buffer, stage, piece, False).wait_send()


def second_order(coef_columns, values, transposed):
    count = lax.axis_size("row")
    quads, rows, cells, cols = values.shape
    whole = pl.BlockSpec(memory_space=pltpu.VMEM)
    return pl.pallas_call(
        functools.partial(step_kernel, count, transposed),
        out_shape=jax.ShapeDtypeStruct(values.shape, jnp.float32),
        in_specs=[whole] * 2,
        out_specs=whole,
        scratch_shapes=[
            pltpu.VMEM((coef_columns.shape[1], cells, cols), jnp.float32),
            pltpu.VMEM((quads, rows, cells, cols), jnp.float32),
            pltpu.VMEM((2, rows + 2, cells + 2 * margin, cols), jnp.float32),
            pltpu.VMEM((2, rows + 2, cells + 2 * margin, cols), jnp.float32),
        ]
        + [pltpu.SemaphoreType.DMA((2 * parts,))] * 4,
        compiler_params=pltpu.CompilerParams(
            collective_id=2 if transposed else 1, has_side_effects=True, vmem_limit_bytes=40 * 2**20
        ),
    )(coef_columns, values)


def reduction(count, part_ref, half_in, half_sum, quarter_in, quarter_sum, piece_in, full, send_sem, recv_sem, peer_send, peer_recv, back_send, back_recv):
    rows = part_ref.shape[0]
    peers = count // 4
    half, quarter, piece = rows // 2, rows // 4, rows // count
    me = lax.axis_index("row")
    low, mid, top = lax.rem(me, 2), lax.rem(me // 2, 2), me // 4
    pair = me + 1 - 2 * low
    across = me + 2 - 4 * mid

    def other(step):
        return lax.rem(top + step, peers)

    def copy_to(source, target, sends, recvs, slot, where):
        return pltpu.make_async_remote_copy(
            src_ref=source,
            dst_ref=target,
            send_sem=sends.at[slot],
            recv_sem=recvs.at[slot],
            device_id={"row": where},
            device_id_type=pl.DeviceIdType.MESH,
        )

    first = copy_to(
        part_ref.at[pl.ds(pl.multiple_of((1 - low) * half, 8), half)], half_in, send_sem, recv_sem, 0, pair
    )
    first.start()
    yield
    first.wait()
    half_sum[...] = part_ref[pl.ds(pl.multiple_of(low * half, 8), half)] + half_in[...]
    second = copy_to(
        half_sum.at[pl.ds(pl.multiple_of((1 - mid) * quarter, 8), quarter)], quarter_in, send_sem, recv_sem, 1, across
    )
    second.start()
    yield
    second.wait()
    quarter_sum[...] = half_sum[pl.ds(pl.multiple_of(mid * quarter, 8), quarter)] + quarter_in[...]
    outgoing = [
        copy_to(
            quarter_sum.at[pl.ds(pl.multiple_of(other(step) * piece, 8), piece)],
            piece_in.at[step],
            peer_send,
            peer_recv,
            step,
            other(step) * 4 + lax.rem(me, 4),
        )
        for step in range(1, peers)
    ]
    for copy in outgoing:
        copy.start()
    yield
    total = quarter_sum[pl.ds(pl.multiple_of(top * piece, 8), piece)]
    for step, copy in enumerate(outgoing, 1):
        copy.wait()
        total = total + piece_in[step]
    base = low * half + mid * quarter
    mine = pl.ds(pl.multiple_of(base + top * piece, 8), piece)
    full[mine] = total
    returning = [
        copy_to(full.at[mine], full.at[mine], back_send, back_recv, step, other(step) * 4 + lax.rem(me, 4))
        for step in range(1, peers)
    ]
    for copy in returning:
        copy.start()
    yield
    for copy in returning:
        copy.wait()
    own_quarter = full.at[pl.ds(pl.multiple_of(base, 8), quarter)]
    third = copy_to(own_quarter, own_quarter, send_sem, recv_sem, 2, across)
    third.start()
    yield
    third.wait()
    own_half = full.at[pl.ds(pl.multiple_of(low * half, 8), half)]
    fourth = copy_to(own_half, own_half, send_sem, recv_sem, 3, pair)
    fourth.start()
    yield
    fourth.wait()


def reduction_scratch(count, rows, cols):
    peers = count // 4
    return [
        pltpu.VMEM((rows // 2, cols), jnp.float32),
        pltpu.VMEM((rows // 2, cols), jnp.float32),
        pltpu.VMEM((rows // 4, cols), jnp.float32),
        pltpu.VMEM((rows // 4, cols), jnp.float32),
        pltpu.VMEM((peers, rows // count, cols), jnp.float32),
        pltpu.VMEM((rows, cols), jnp.float32),
        pltpu.SemaphoreType.DMA((4,)),
        pltpu.SemaphoreType.DMA((4,)),
    ] + [pltpu.SemaphoreType.DMA((peers,))] * 4


tile = 32


def tile_inverse(block):
    shape = (tile, tile)
    row_ids = lax.broadcasted_iota(jnp.int32, shape, 0)
    col_ids = lax.broadcasted_iota(jnp.int32, shape, 1)
    right = (row_ids == col_ids).astype(jnp.float32)
    left = block
    scale = jnp.zeros(shape, jnp.float32)
    for start in range(0, tile, 8):
        columns = [
            jnp.broadcast_to(left[start:, start + k : start + k + 1], (tile - start, tile)) for k in range(8)
        ]
        below_left, below_right = left[start:], right[start:]
        ids = row_ids[start:]
        for j in range(8):
            pivot = columns[j][j : j + 1]
            factor = jnp.where(ids > start + j, columns[j] * (1.0 / pivot), 0.0)
            scale = jnp.where(row_ids == start + j, lax.rsqrt(pivot), scale)
            for k in range(j + 1, 8):
                columns[k] = columns[k] - factor * columns[k][j : j + 1]
            below_left = below_left - factor * below_left[j : j + 1]
            below_right = below_right - factor * below_right[j : j + 1]
        if start:
            left = jnp.concatenate([left[:start], below_left], axis=0)
            right = jnp.concatenate([right[:start], below_right], axis=0)
        else:
            left, right = below_left, below_right
    return right * scale


def mul(a, b, contract):
    return lax.dot_general(a, b, ((contract[0:1], contract[1:2]), ((), ())), precision=exact, preferred_element_type=jnp.float32)


def factor_kernel(count, product_ref, bar_ref, inv_ref, mix_ref, work, gram_part, cross_part, *scratch):
    size = bar_ref.shape[0]
    side = size // 2
    gram_scratch, cross_scratch = scratch[:12], scratch[12:]
    gram_full, cross_full = gram_scratch[5], cross_scratch[5]
    me = lax.axis_index("row")
    low, mid, top = lax.rem(me, 2), lax.rem(me // 2, 2), me // 4
    peers = count // 4
    barrier = pltpu.get_barrier_semaphore()
    friends = [me + 1 - 2 * low, me + 2 - 4 * mid]
    friends += [lax.rem(top + step, peers) * 4 + lax.rem(me, 4) for step in range(1, peers)]
    for friend in friends:
        pl.semaphore_signal(barrier, inc=1, device_id={"row": friend}, device_id_type=pl.DeviceIdType.MESH)
    gram_part[:side] = product_ref[:side, :side]
    gram_part[side:size] = product_ref[side:size, :side]
    gram_part[size : size + side] = product_ref[side:size, side:]
    if gram_part.shape[0] > size + side:
        gram_part[size + side :] = jnp.zeros((gram_part.shape[0] - size - side, side), jnp.float32)
    cross_part[:size] = product_ref[size:, :side]
    cross_part[size:] = product_ref[size:, side:]
    pl.semaphore_wait(barrier, len(friends))
    gram_steps = reduction(count, gram_part, *gram_scratch)
    cross_steps = reduction(count, cross_part, *cross_scratch)
    next(gram_steps)
    next(gram_steps)
    next(cross_steps)
    next(gram_steps)
    next(cross_steps)
    next(gram_steps)
    next(gram_steps)
    next(gram_steps)
    next(cross_steps)
    next(gram_steps, None)

    row_ids = lax.broadcasted_iota(jnp.int32, (size, size), 0)
    col_ids = lax.broadcasted_iota(jnp.int32, (size, size), 1)
    work[:side, :side] = gram_full[:side]
    work[side:, :side] = gram_full[side:size]
    work[:side, side:size] = gram_full[side:size].T
    work[side:, side:size] = gram_full[size : size + side]
    work[:, size:] = (row_ids == col_ids).astype(jnp.float32)
    for index, start in enumerate(range(0, size, tile)):
        stop = start + tile
        small = tile_inverse(work[start:stop, start:stop])
        panel = mul(small, work[start:stop, :], (1, 0))
        work[start:stop, :] = panel
        if stop < size:
            update = mul(panel[:, :size].T, panel, (1, 0))
            work[stop:, :] = work[stop:, :] - update[stop:]
        if index in (1, 3, 5):
            next(cross_steps)
    upper = jnp.where(row_ids <= col_ids, work[:, :size], 0.0)
    inverse = jnp.where(row_ids >= col_ids, work[:, size:], 0.0)
    inv_ref[...] = inverse
    bar = jnp.where(row_ids <= col_ids, bar_ref[...], 0.0)
    target = mul(upper, bar, (1, 1))
    next(cross_steps, None)
    cross = jnp.concatenate([cross_full[:size], cross_full[size:]], axis=1)
    middle = target - mul(cross, inverse, (1, 1))
    symmetric = jnp.where(row_ids >= col_ids, middle, middle.T)
    mix_ref[...] = mul(inverse.T, mul(symmetric, inverse, (1, 0)), (1, 0))


def factor(products, r_bar):
    count = lax.axis_size("row")
    size = r_bar.shape[0]
    side = size // 2
    unit = 8 * count
    gram_rows = (size + side + unit - 1) // unit * unit
    shape = jax.ShapeDtypeStruct((size, size), jnp.float32)
    whole = pl.BlockSpec(memory_space=pltpu.VMEM)
    return pl.pallas_call(
        functools.partial(factor_kernel, count),
        out_shape=(shape, shape),
        in_specs=[whole] * 2,
        out_specs=(whole, whole),
        scratch_shapes=[
            pltpu.VMEM((size, 2 * size), jnp.float32),
            pltpu.VMEM((gram_rows, side), jnp.float32),
            pltpu.VMEM((2 * size, side), jnp.float32),
        ]
        + reduction_scratch(count, gram_rows, side)
        + reduction_scratch(count, 2 * size, side),
        compiler_params=pltpu.CompilerParams(collective_id=0, has_side_effects=True, vmem_limit_bytes=24 * 2**20),
    )(products, r_bar)


def halves(value):
    high = value.astype(jnp.bfloat16)
    return high, (value - high.astype(jnp.float32)).astype(jnp.bfloat16)


def three(left, high, low):
    left_high, left_low = halves(left)
    dot = functools.partial(jnp.dot, preferred_element_type=jnp.float32)
    return dot(left_high, high) + (dot(left_high, low) + dot(left_low, high))


def grad_kernel(bar_ref, z_ref, noise_ref, inv_ref, mix_ref, z_out, noise_out, inv_high, inv_low, mix_high, mix_low):
    @pl.when(pl.program_id(0) == 0)
    def _():
        inv_high[...], inv_low[...] = halves(inv_ref[...])
        mix_high[...], mix_low[...] = halves(mix_ref[...])

    stacked = jnp.concatenate([z_ref[...], noise_ref[...]], axis=1)
    grad = three(bar_ref[...], inv_high[...], inv_low[...]) + three(stacked, mix_high[...], mix_low[...])
    z_out[...] = grad[:, : z_out.shape[1]]
    noise_out[...] = grad[:, z_out.shape[1] :]


def gradient(bar_rows, z_rows, noise_rows, inverse, mix):
    rows, size = bar_rows.shape
    block = rows // 8
    square = pl.BlockSpec((size, size), lambda i: (0, 0))

    def strip(value):
        return pl.BlockSpec((block, value.shape[1]), lambda i: (i, 0))

    return pl.pallas_call(
        grad_kernel,
        grid=(8,),
        out_shape=(
            jax.ShapeDtypeStruct(z_rows.shape, jnp.float32),
            jax.ShapeDtypeStruct(noise_rows.shape, jnp.float32),
        ),
        in_specs=[strip(bar_rows), strip(z_rows), strip(noise_rows), square, square],
        out_specs=(strip(z_rows), strip(noise_rows)),
        scratch_shapes=[pltpu.VMEM((size, size), jnp.bfloat16)] * 4,
        compiler_params=pltpu.CompilerParams(vmem_limit_bytes=24 * 2**20),
    )(bar_rows, z_rows, noise_rows, inverse, mix)


def on_device(cell_coeffs, z_factor, noise_cols, q_bar, r_bar):
    scaled = cell_coeffs * jnp.array(rate_scales, jnp.float32)[:, None, None]
    rank_cols = z_factor.shape[3]
    coef_columns = scaled.reshape(-1, scaled.shape[2]).T

    z_rows = second_order(coef_columns, z_factor, False).reshape(-1, rank_cols)
    noise_rows = noise_cols.reshape(-1, noise_cols.shape[3])
    flat_rows = jnp.concatenate([z_rows, noise_rows], axis=1)
    bar_rows = q_bar.reshape(-1, q_bar.shape[3])
    both = jnp.concatenate([flat_rows, bar_rows], axis=1)
    products = lax.dot_general(both, flat_rows, (((0,), (0,)), ((), ())), precision=lax.Precision.HIGH)
    inverse, mix = factor(products, r_bar)
    z_part, noise_part = gradient(bar_rows, z_rows, noise_rows, inverse, mix)
    z_grad = second_order(coef_columns, z_part.reshape(z_factor.shape), True)
    return (z_grad, noise_part.reshape(noise_cols.shape))


def solution(mesh):
    return jax.shard_map(
        on_device,
        mesh=mesh,
        in_specs=(
            P(None, "row", None),
            P(None, ("grp", "row"), None, None),
            P(None, ("grp", "row"), None, None),
            P(None, ("grp", "row"), None, None),
            P("grp", None),
        ),
        out_specs=(P(None, ("grp", "row"), None, None), P(None, ("grp", "row"), None, None)),
        check_vma=False,
    )
```

```python
import functools

import jax
import jax.numpy as jnp
from jax import lax
from jax.experimental import pallas as pl
from jax.experimental.pallas import tpu as pltpu
from jax.sharding import PartitionSpec as P

rate_scales = (0.4, 0.4, 0.1, 0.2, 0.1, 0.1)
exact = lax.Precision.HIGHEST


parts = 4
margin = 8


def step_kernel(count, transposed, coef_ref, value_ref, out_ref, coefs, first, source, source_two, send_low, recv_low, send_high, recv_high):
    rows, cells, cols = value_ref.shape[1:]
    chunk = cells // parts
    me = lax.axis_index("row")
    has_low, has_high = me > 0, me < count - 1

    def link(buffer, stage, piece, upward):
        cut = pl.ds(margin + piece * chunk, chunk)
        sends, recvs = (send_high, recv_high) if upward else (send_low, recv_low)
        slot = stage * parts + piece
        return pltpu.make_async_remote_copy(
            src_ref=buffer.at[:, rows if upward else 1, cut],
            dst_ref=buffer.at[:, 0 if upward else rows + 1, cut],
            send_sem=sends.at[slot],
            recv_sem=recvs.at[slot],
            device_id={"row": me + 1 if upward else me - 1},
            device_id_type=pl.DeviceIdType.MESH,
        )

    def send(buffer, stage, piece):
        @pl.when(has_high)
        def _():
            link(buffer, stage, piece, True).start()

        @pl.when(has_low)
        def _():
            link(buffer, stage, piece, False).start()

    def receive(buffer, stage, piece):
        @pl.when(has_low)
        def _():
            link(buffer, stage, piece, True).wait_recv()

        @pl.when(has_high)
        def _():
            link(buffer, stage, piece, False).wait_recv()

    barrier = pltpu.get_barrier_semaphore()

    @pl.when(has_low)
    def _():
        pl.semaphore_signal(barrier, inc=1, device_id={"row": me - 1}, device_id_type=pl.DeviceIdType.MESH)

    @pl.when(has_high)
    def _():
        pl.semaphore_signal(barrier, inc=1, device_id={"row": me + 1}, device_id_type=pl.DeviceIdType.MESH)

    def coef(kind, row, piece):
        return coefs[kind * rows + row, piece * chunk : (piece + 1) * chunk]

    def at(piece):
        return slice(piece * chunk, (piece + 1) * chunk)

    def inner(piece, shift=0):
        return slice(margin + piece * chunk + shift, margin + (piece + 1) * chunk + shift)

    def spread(kind):
        for row in range(rows):
            index = kind * rows + row
            coefs[index] = jnp.broadcast_to(coef_ref[:, index : index + 1], (cells, cols))

    def fill(buffer, values, piece):
        for row in range(rows):
            for quad in range(2):
                value = values[quad, row, at(piece)]
                if transposed:
                    value = value * coef(5, row, piece)
                buffer[quad, row + 1, inner(piece)] = value

    def zero_rim(buffer):
        for quad in range(2):
            for row in range(rows):
                buffer[quad, row + 1, :margin] = jnp.zeros((margin, cols), jnp.float32)
                buffer[quad, row + 1, margin + cells :] = jnp.zeros((margin, cols), jnp.float32)

        @pl.when(jnp.logical_not(has_low))
        def _():
            buffer[:, 0] = jnp.zeros(buffer.shape[:1] + buffer.shape[2:], jnp.float32)

        @pl.when(jnp.logical_not(has_high))
        def _():
            buffer[:, rows + 1] = jnp.zeros(buffer.shape[:1] + buffer.shape[2:], jnp.float32)

    def local(values, buffer, row, piece):
        xa, pa, xb, pb = [values[quad, row, at(piece)] for quad in range(4)]
        detuning, mech, coupling, cavity, phonon, hopping = [coef(kind, row, piece) for kind in range(6)]
        sums = []
        for quad in range(2):
            total = buffer[quad, row + 1, inner(piece, -1)] + buffer[quad, row + 1, inner(piece, 1)]
            if row > 0:
                total = total + buffer[quad, row, inner(piece)]
            if row < rows - 1:
                total = total + buffer[quad, row + 2, inner(piece)]
            sums.append(total)
        if transposed:
            return (
                -0.5 * cavity * xa + detuning * pa - 2.0 * coupling * pb + sums[1],
                -detuning * xa - 0.5 * cavity * pa - sums[0],
                -2.0 * coupling * pa - mech * pb,
                mech * xb - 0.5 * phonon * pb,
            )
        return (
            -0.5 * cavity * xa - detuning * pa - hopping * sums[1],
            detuning * xa - 0.5 * cavity * pa - 2.0 * coupling * xb + hopping * sums[0],
            mech * pb,
            -mech * xb - 0.5 * phonon * pb - 2.0 * coupling * xa,
        )

    def edges(buffer, piece):
        found = []
        for row, halo in ((0, 0), (rows - 1, rows + 1)):
            light_x, light_p = buffer[0, halo, inner(piece)], buffer[1, halo, inner(piece)]
            if transposed:
                found.append((row, light_p, -light_x))
            else:
                hopping = coef(5, row, piece)
                found.append((row, -hopping * light_p, hopping * light_x))
        return found

    spread(5)
    fill(source, value_ref, 0)

    pl.semaphore_wait(barrier, jnp.where(me > 0, 1, 0) + jnp.where(me < count - 1, 1, 0))

    send(source, 0, 0)
    for piece in range(1, parts):
        fill(source, value_ref, piece)
        send(source, 0, piece)
    zero_rim(source)
    zero_rim(source_two)
    for kind in range(5):
        spread(kind)
    for piece in range(parts):
        for row in range(rows):
            for quad, value in enumerate(local(value_ref, source, row, piece)):
                first[quad, row, at(piece)] = value
    for piece in range(parts):
        receive(source, 0, piece)
        for row, add_x, add_p in edges(source, piece):
            first[0, row, at(piece)] = first[0, row, at(piece)] + add_x
            first[1, row, at(piece)] = first[1, row, at(piece)] + add_p
        fill(source_two, first, piece)
        send(source_two, 1, piece)
    for piece in range(parts):
        for row in range(rows):
            for quad, value in enumerate(local(first, source_two, row, piece)):
                out_ref[quad, row, at(piece)] = (
                    value_ref[quad, row, at(piece)] + first[quad, row, at(piece)] + 0.5 * value
                )
    for piece in range(parts):
        receive(source_two, 1, piece)
        for row, add_x, add_p in edges(source_two, piece):
            out_ref[0, row, at(piece)] = out_ref[0, row, at(piece)] + 0.5 * add_x
            out_ref[1, row, at(piece)] = out_ref[1, row, at(piece)] + 0.5 * add_p
    for stage, buffer in enumerate((source, source_two)):
        for piece in range(parts):

            @pl.when(has_high)
            def _():
                link(buffer, stage, piece, True).wait_send()

            @pl.when(has_low)
            def _():
                link(buffer, stage, piece, False).wait_send()


def second_order(coef_columns, values, transposed):
    count = lax.axis_size("row")
    quads, rows, cells, cols = values.shape
    whole = pl.BlockSpec(memory_space=pltpu.VMEM)
    return pl.pallas_call(
        functools.partial(step_kernel, count, transposed),
        out_shape=jax.ShapeDtypeStruct(values.shape, jnp.float32),
        in_specs=[whole] * 2,
        out_specs=whole,
        scratch_shapes=[
            pltpu.VMEM((coef_columns.shape[1], cells, cols), jnp.float32),
            pltpu.VMEM((quads, rows, cells, cols), jnp.float32),
            pltpu.VMEM((2, rows + 2, cells + 2 * margin, cols), jnp.float32),
            pltpu.VMEM((2, rows + 2, cells + 2 * margin, cols), jnp.float32),
        ]
        + [pltpu.SemaphoreType.DMA((2 * parts,))] * 4,
        compiler_params=pltpu.CompilerParams(
            collective_id=2 if transposed else 1, has_side_effects=True, vmem_limit_bytes=40 * 2**20
        ),
    )(coef_columns, values)


def reduction(count, part_ref, half_in, half_sum, quarter_in, quarter_sum, piece_in, full, send_sem, recv_sem, peer_send, peer_recv, back_send, back_recv):
    rows = part_ref.shape[0]
    peers = count // 4
    half, quarter, piece = rows // 2, rows // 4, rows // count
    me = lax.axis_index("row")
    low, mid, top = lax.rem(me, 2), lax.rem(me // 2, 2), me // 4
    pair = me + 1 - 2 * low
    across = me + 2 - 4 * mid

    def other(step):
        return lax.rem(top + step, peers)

    def copy_to(source, target, sends, recvs, slot, where):
        return pltpu.make_async_remote_copy(
            src_ref=source,
            dst_ref=target,
            send_sem=sends.at[slot],
            recv_sem=recvs.at[slot],
            device_id={"row": where},
            device_id_type=pl.DeviceIdType.MESH,
        )

    first = copy_to(
        part_ref.at[pl.ds(pl.multiple_of((1 - low) * half, 8), half)], half_in, send_sem, recv_sem, 0, pair
    )
    first.start()
    yield
    first.wait()
    half_sum[...] = part_ref[pl.ds(pl.multiple_of(low * half, 8), half)] + half_in[...]
    second = copy_to(
        half_sum.at[pl.ds(pl.multiple_of((1 - mid) * quarter, 8), quarter)], quarter_in, send_sem, recv_sem, 1, across
    )
    second.start()
    yield
    second.wait()
    quarter_sum[...] = half_sum[pl.ds(pl.multiple_of(mid * quarter, 8), quarter)] + quarter_in[...]
    outgoing = [
        copy_to(
            quarter_sum.at[pl.ds(pl.multiple_of(other(step) * piece, 8), piece)],
            piece_in.at[step],
            peer_send,
            peer_recv,
            step,
            other(step) * 4 + lax.rem(me, 4),
        )
        for step in range(1, peers)
    ]
    for copy in outgoing:
        copy.start()
    yield
    total = quarter_sum[pl.ds(pl.multiple_of(top * piece, 8), piece)]
    for step, copy in enumerate(outgoing, 1):
        copy.wait()
        total = total + piece_in[step]
    base = low * half + mid * quarter
    mine = pl.ds(pl.multiple_of(base + top * piece, 8), piece)
    full[mine] = total
    returning = [
        copy_to(full.at[mine], full.at[mine], back_send, back_recv, step, other(step) * 4 + lax.rem(me, 4))
        for step in range(1, peers)
    ]
    for copy in returning:
        copy.start()
    yield
    for copy in returning:
        copy.wait()
    own_quarter = full.at[pl.ds(pl.multiple_of(base, 8), quarter)]
    third = copy_to(own_quarter, own_quarter, send_sem, recv_sem, 2, across)
    third.start()
    yield
    third.wait()
    own_half = full.at[pl.ds(pl.multiple_of(low * half, 8), half)]
    fourth = copy_to(own_half, own_half, send_sem, recv_sem, 3, pair)
    fourth.start()
    yield
    fourth.wait()


def direct_reduction(count, part_ref, piece_in, full, peer_send, peer_recv, back_send, back_recv):
    piece = part_ref.shape[0] // count
    me = lax.axis_index("row")
    others = [lax.rem(me + step, count) for step in range(1, count)]
    mine = pl.ds(pl.multiple_of(me * piece, 8), piece)

    def copy_to(source, target, sends, recvs, step):
        return pltpu.make_async_remote_copy(
            src_ref=source,
            dst_ref=target,
            send_sem=sends.at[step],
            recv_sem=recvs.at[step],
            device_id={"row": others[step - 1]},
            device_id_type=pl.DeviceIdType.MESH,
        )

    outgoing = [
        copy_to(
            part_ref.at[pl.ds(pl.multiple_of(other * piece, 8), piece)], piece_in.at[step], peer_send, peer_recv, step
        )
        for step, other in enumerate(others, 1)
    ]
    for copy in outgoing:
        copy.start()
    yield
    total = part_ref[mine]
    for step, copy in enumerate(outgoing, 1):
        copy.wait()
        total = total + piece_in[step]
    full[mine] = total
    returning = [copy_to(full.at[mine], full.at[mine], back_send, back_recv, step) for step in range(1, count)]
    for copy in returning:
        copy.start()
    yield
    for copy in returning:
        copy.wait()


def direct_scratch(count, rows, cols):
    return [
        pltpu.VMEM((count, rows // count, cols), jnp.float32),
        pltpu.VMEM((rows, cols), jnp.float32),
    ] + [pltpu.SemaphoreType.DMA((count,))] * 4


def reduction_scratch(count, rows, cols):
    peers = count // 4
    return [
        pltpu.VMEM((rows // 2, cols), jnp.float32),
        pltpu.VMEM((rows // 2, cols), jnp.float32),
        pltpu.VMEM((rows // 4, cols), jnp.float32),
        pltpu.VMEM((rows // 4, cols), jnp.float32),
        pltpu.VMEM((peers, rows // count, cols), jnp.float32),
        pltpu.VMEM((rows, cols), jnp.float32),
        pltpu.SemaphoreType.DMA((4,)),
        pltpu.SemaphoreType.DMA((4,)),
    ] + [pltpu.SemaphoreType.DMA((peers,))] * 4


tile = 32


def tile_inverse(block):
    shape = (tile, tile)
    row_ids = lax.broadcasted_iota(jnp.int32, shape, 0)
    col_ids = lax.broadcasted_iota(jnp.int32, shape, 1)
    right = (row_ids == col_ids).astype(jnp.float32)
    left = block
    scale = jnp.zeros(shape, jnp.float32)
    for start in range(0, tile, 8):
        columns = [
            jnp.broadcast_to(left[start:, start + k : start + k + 1], (tile - start, tile)) for k in range(8)
        ]
        below_left, below_right = left[start:], right[start:]
        ids = row_ids[start:]
        for j in range(8):
            pivot = columns[j][j : j + 1]
            factor = jnp.where(ids > start + j, columns[j] * (1.0 / pivot), 0.0)
            scale = jnp.where(row_ids == start + j, lax.rsqrt(pivot), scale)
            for k in range(j + 1, 8):
                columns[k] = columns[k] - factor * columns[k][j : j + 1]
            below_left = below_left - factor * below_left[j : j + 1]
            below_right = below_right - factor * below_right[j : j + 1]
        if start:
            left = jnp.concatenate([left[:start], below_left], axis=0)
            right = jnp.concatenate([right[:start], below_right], axis=0)
        else:
            left, right = below_left, below_right
    return right * scale


def mul(a, b, contract):
    return lax.dot_general(a, b, ((contract[0:1], contract[1:2]), ((), ())), precision=exact, preferred_element_type=jnp.float32)


def factor_kernel(count, product_ref, bar_ref, inv_ref, mix_ref, work, gram_part, cross_part, *scratch):
    size = bar_ref.shape[0]
    side = size // 2
    gram_scratch, cross_scratch = scratch[:6], scratch[6:]
    gram_full, cross_full = gram_scratch[1], cross_scratch[5]
    me = lax.axis_index("row")
    barrier = pltpu.get_barrier_semaphore()
    friends = [lax.rem(me + step, count) for step in range(1, count)]
    for friend in friends:
        pl.semaphore_signal(barrier, inc=1, device_id={"row": friend}, device_id_type=pl.DeviceIdType.MESH)
    gram_part[:side] = product_ref[:side, :side]
    gram_part[side:size] = product_ref[side:size, :side]
    gram_part[size : size + side] = product_ref[side:size, side:]
    if gram_part.shape[0] > size + side:
        gram_part[size + side :] = jnp.zeros((gram_part.shape[0] - size - side, side), jnp.float32)
    cross_part[:size] = product_ref[size:, :side]
    cross_part[size:] = product_ref[size:, side:]
    pl.semaphore_wait(barrier, len(friends))
    gram_steps = direct_reduction(count, gram_part, *gram_scratch)
    cross_steps = reduction(count, cross_part, *cross_scratch)
    next(gram_steps)
    next(cross_steps)
    next(gram_steps)
    next(gram_steps, None)
    next(cross_steps)

    row_ids = lax.broadcasted_iota(jnp.int32, (size, size), 0)
    col_ids = lax.broadcasted_iota(jnp.int32, (size, size), 1)
    work[:side, :side] = gram_full[:side]
    work[side:, :side] = gram_full[side:size]
    work[:side, side:size] = gram_full[side:size].T
    work[side:, side:size] = gram_full[size : size + side]
    work[:, size:] = (row_ids == col_ids).astype(jnp.float32)
    for index, start in enumerate(range(0, size, tile)):
        stop = start + tile
        small = tile_inverse(work[start:stop, start:stop])
        panel = mul(small, work[start:stop, :], (1, 0))
        work[start:stop, :] = panel
        if stop < size:
            update = mul(panel[:, :size].T, panel, (1, 0))
            work[stop:, :] = work[stop:, :] - update[stop:]
        if index in (1, 3, 4, 6):
            next(cross_steps)
    upper = jnp.where(row_ids <= col_ids, work[:, :size], 0.0)
    inverse = jnp.where(row_ids >= col_ids, work[:, size:], 0.0)
    inv_ref[...] = inverse
    bar = jnp.where(row_ids <= col_ids, bar_ref[...], 0.0)
    target = mul(upper, bar, (1, 1))
    next(cross_steps, None)
    cross = jnp.concatenate([cross_full[:size], cross_full[size:]], axis=1)
    middle = target - mul(cross, inverse, (1, 1))
    symmetric = jnp.where(row_ids >= col_ids, middle, middle.T)
    mix_ref[...] = mul(inverse.T, mul(symmetric, inverse, (1, 0)), (1, 0))


def factor(products, r_bar):
    count = lax.axis_size("row")
    size = r_bar.shape[0]
    side = size // 2
    unit = 8 * count
    gram_rows = (size + side + unit - 1) // unit * unit
    shape = jax.ShapeDtypeStruct((size, size), jnp.float32)
    whole = pl.BlockSpec(memory_space=pltpu.VMEM)
    return pl.pallas_call(
        functools.partial(factor_kernel, count),
        out_shape=(shape, shape),
        in_specs=[whole] * 2,
        out_specs=(whole, whole),
        scratch_shapes=[
            pltpu.VMEM((size, 2 * size), jnp.float32),
            pltpu.VMEM((gram_rows, side), jnp.float32),
            pltpu.VMEM((2 * size, side), jnp.float32),
        ]
        + direct_scratch(count, gram_rows, side)
        + reduction_scratch(count, 2 * size, side),
        compiler_params=pltpu.CompilerParams(collective_id=0, has_side_effects=True, vmem_limit_bytes=24 * 2**20),
    )(products, r_bar)


def halves(value):
    high = value.astype(jnp.bfloat16)
    return high, (value - high.astype(jnp.float32)).astype(jnp.bfloat16)


def three(left, high, low):
    left_high, left_low = halves(left)
    dot = functools.partial(jnp.dot, preferred_element_type=jnp.float32)
    return dot(left_high, high) + (dot(left_high, low) + dot(left_low, high))


def grad_kernel(bar_ref, z_ref, noise_ref, inv_ref, mix_ref, z_out, noise_out, inv_high, inv_low, mix_high, mix_low):
    @pl.when(pl.program_id(0) == 0)
    def _():
        inv_high[...], inv_low[...] = halves(inv_ref[...])
        mix_high[...], mix_low[...] = halves(mix_ref[...])

    stacked = jnp.concatenate([z_ref[...], noise_ref[...]], axis=1)
    grad = three(bar_ref[...], inv_high[...], inv_low[...]) + three(stacked, mix_high[...], mix_low[...])
    z_out[...] = grad[:, : z_out.shape[1]]
    noise_out[...] = grad[:, z_out.shape[1] :]


def gradient(bar_rows, z_rows, noise_rows, inverse, mix):
    rows, size = bar_rows.shape
    block = rows // 8
    square = pl.BlockSpec((size, size), lambda i: (0, 0))

    def strip(value):
        return pl.BlockSpec((block, value.shape[1]), lambda i: (i, 0))

    return pl.pallas_call(
        grad_kernel,
        grid=(8,),
        out_shape=(
            jax.ShapeDtypeStruct(z_rows.shape, jnp.float32),
            jax.ShapeDtypeStruct(noise_rows.shape, jnp.float32),
        ),
        in_specs=[strip(bar_rows), strip(z_rows), strip(noise_rows), square, square],
        out_specs=(strip(z_rows), strip(noise_rows)),
        scratch_shapes=[pltpu.VMEM((size, size), jnp.bfloat16)] * 4,
        compiler_params=pltpu.CompilerParams(vmem_limit_bytes=24 * 2**20),
    )(bar_rows, z_rows, noise_rows, inverse, mix)


def on_device(cell_coeffs, z_factor, noise_cols, q_bar, r_bar):
    scaled = cell_coeffs * jnp.array(rate_scales, jnp.float32)[:, None, None]
    rank_cols = z_factor.shape[3]
    coef_columns = scaled.reshape(-1, scaled.shape[2]).T

    z_rows = second_order(coef_columns, z_factor, False).reshape(-1, rank_cols)
    noise_rows = noise_cols.reshape(-1, noise_cols.shape[3])
    flat_rows = jnp.concatenate([z_rows, noise_rows], axis=1)
    bar_rows = q_bar.reshape(-1, q_bar.shape[3])
    both = jnp.concatenate([flat_rows, bar_rows], axis=1)
    products = lax.dot_general(both, flat_rows, (((0,), (0,)), ((), ())), precision=lax.Precision.HIGH)
    inverse, mix = factor(products, r_bar)
    z_part, noise_part = gradient(bar_rows, z_rows, noise_rows, inverse, mix)
    z_grad = second_order(coef_columns, z_part.reshape(z_factor.shape), True)
    return (z_grad, noise_part.reshape(noise_cols.shape))


def solution(mesh):
    return jax.shard_map(
        on_device,
        mesh=mesh,
        in_specs=(
            P(None, "row", None),
            P(None, ("grp", "row"), None, None),
            P(None, ("grp", "row"), None, None),
            P(None, ("grp", "row"), None, None),
            P("grp", None),
        ),
        out_specs=(P(None, ("grp", "row"), None, None), P(None, ("grp", "row"), None, None)),
        check_vma=False,
    )
```

```python
import functools

import jax
import jax.numpy as jnp
from jax import lax
from jax.experimental import pallas as pl
from jax.experimental.pallas import tpu as pltpu
from jax.sharding import PartitionSpec as P

rate_scales = (0.4, 0.4, 0.1, 0.2, 0.1, 0.1)
exact = lax.Precision.HIGHEST


parts = 4
margin = 8


def step_kernel(count, transposed, coef_ref, value_ref, out_ref, coefs, first, source, source_two, send_low, recv_low, send_high, recv_high):
    rows, cells, cols = value_ref.shape[1:]
    chunk = cells // parts
    me = lax.axis_index("row")
    has_low, has_high = me > 0, me < count - 1

    def link(buffer, stage, piece, upward):
        cut = pl.ds(margin + piece * chunk, chunk)
        sends, recvs = (send_high, recv_high) if upward else (send_low, recv_low)
        slot = stage * parts + piece
        return pltpu.make_async_remote_copy(
            src_ref=buffer.at[:, rows if upward else 1, cut],
            dst_ref=buffer.at[:, 0 if upward else rows + 1, cut],
            send_sem=sends.at[slot],
            recv_sem=recvs.at[slot],
            device_id={"row": me + 1 if upward else me - 1},
            device_id_type=pl.DeviceIdType.MESH,
        )

    def send(buffer, stage, piece):
        @pl.when(has_high)
        def _():
            link(buffer, stage, piece, True).start()

        @pl.when(has_low)
        def _():
            link(buffer, stage, piece, False).start()

    def receive(buffer, stage, piece):
        @pl.when(has_low)
        def _():
            link(buffer, stage, piece, True).wait_recv()

        @pl.when(has_high)
        def _():
            link(buffer, stage, piece, False).wait_recv()

    barrier = pltpu.get_barrier_semaphore()

    @pl.when(has_low)
    def _():
        pl.semaphore_signal(barrier, inc=1, device_id={"row": me - 1}, device_id_type=pl.DeviceIdType.MESH)

    @pl.when(has_high)
    def _():
        pl.semaphore_signal(barrier, inc=1, device_id={"row": me + 1}, device_id_type=pl.DeviceIdType.MESH)

    def coef(kind, row, piece):
        return coefs[kind * rows + row, piece * chunk : (piece + 1) * chunk]

    def at(piece):
        return slice(piece * chunk, (piece + 1) * chunk)

    def inner(piece, shift=0):
        return slice(margin + piece * chunk + shift, margin + (piece + 1) * chunk + shift)

    def spread(kind):
        for row in range(rows):
            index = kind * rows + row
            coefs[index] = jnp.broadcast_to(coef_ref[:, index : index + 1], (cells, cols))

    def fill(buffer, values, piece):
        for row in range(rows):
            for quad in range(2):
                value = values[quad, row, at(piece)]
                if transposed:
                    value = value * coef(5, row, piece)
                buffer[quad, row + 1, inner(piece)] = value

    def zero_rim(buffer):
        for quad in range(2):
            for row in range(rows):
                buffer[quad, row + 1, :margin] = jnp.zeros((margin, cols), jnp.float32)
                buffer[quad, row + 1, margin + cells :] = jnp.zeros((margin, cols), jnp.float32)

        @pl.when(jnp.logical_not(has_low))
        def _():
            buffer[:, 0] = jnp.zeros(buffer.shape[:1] + buffer.shape[2:], jnp.float32)

        @pl.when(jnp.logical_not(has_high))
        def _():
            buffer[:, rows + 1] = jnp.zeros(buffer.shape[:1] + buffer.shape[2:], jnp.float32)

    def local(values, buffer, row, piece):
        xa, pa, xb, pb = [values[quad, row, at(piece)] for quad in range(4)]
        detuning, mech, coupling, cavity, phonon, hopping = [coef(kind, row, piece) for kind in range(6)]
        sums = []
        for quad in range(2):
            total = buffer[quad, row + 1, inner(piece, -1)] + buffer[quad, row + 1, inner(piece, 1)]
            if row > 0:
                total = total + buffer[quad, row, inner(piece)]
            if row < rows - 1:
                total = total + buffer[quad, row + 2, inner(piece)]
            sums.append(total)
        if transposed:
            return (
                -0.5 * cavity * xa + detuning * pa - 2.0 * coupling * pb + sums[1],
                -detuning * xa - 0.5 * cavity * pa - sums[0],
                -2.0 * coupling * pa - mech * pb,
                mech * xb - 0.5 * phonon * pb,
            )
        return (
            -0.5 * cavity * xa - detuning * pa - hopping * sums[1],
            detuning * xa - 0.5 * cavity * pa - 2.0 * coupling * xb + hopping * sums[0],
            mech * pb,
            -mech * xb - 0.5 * phonon * pb - 2.0 * coupling * xa,
        )

    def edges(buffer, piece):
        found = []
        for row, halo in ((0, 0), (rows - 1, rows + 1)):
            light_x, light_p = buffer[0, halo, inner(piece)], buffer[1, halo, inner(piece)]
            if transposed:
                found.append((row, light_p, -light_x))
            else:
                hopping = coef(5, row, piece)
                found.append((row, -hopping * light_p, hopping * light_x))
        return found

    spread(5)
    fill(source, value_ref, 0)

    pl.semaphore_wait(barrier, jnp.where(me > 0, 1, 0) + jnp.where(me < count - 1, 1, 0))

    send(source, 0, 0)
    for piece in range(1, parts):
        fill(source, value_ref, piece)
        send(source, 0, piece)
    zero_rim(source)
    zero_rim(source_two)
    for kind in range(5):
        spread(kind)
    for piece in range(parts):
        for row in range(rows):
            for quad, value in enumerate(local(value_ref, source, row, piece)):
                first[quad, row, at(piece)] = value
    for piece in range(parts):
        receive(source, 0, piece)
        for row, add_x, add_p in edges(source, piece):
            first[0, row, at(piece)] = first[0, row, at(piece)] + add_x
            first[1, row, at(piece)] = first[1, row, at(piece)] + add_p
        fill(source_two, first, piece)
        send(source_two, 1, piece)
    for piece in range(parts):
        for row in range(rows):
            for quad, value in enumerate(local(first, source_two, row, piece)):
                out_ref[quad, row, at(piece)] = (
                    value_ref[quad, row, at(piece)] + first[quad, row, at(piece)] + 0.5 * value
                )
    for piece in range(parts):
        receive(source_two, 1, piece)
        for row, add_x, add_p in edges(source_two, piece):
            out_ref[0, row, at(piece)] = out_ref[0, row, at(piece)] + 0.5 * add_x
            out_ref[1, row, at(piece)] = out_ref[1, row, at(piece)] + 0.5 * add_p
    for stage, buffer in enumerate((source, source_two)):
        for piece in range(parts):

            @pl.when(has_high)
            def _():
                link(buffer, stage, piece, True).wait_send()

            @pl.when(has_low)
            def _():
                link(buffer, stage, piece, False).wait_send()


def second_order(coef_columns, values, transposed):
    count = lax.axis_size("row")
    quads, rows, cells, cols = values.shape
    whole = pl.BlockSpec(memory_space=pltpu.VMEM)
    return pl.pallas_call(
        functools.partial(step_kernel, count, transposed),
        out_shape=jax.ShapeDtypeStruct(values.shape, jnp.float32),
        in_specs=[whole] * 2,
        out_specs=whole,
        scratch_shapes=[
            pltpu.VMEM((coef_columns.shape[1], cells, cols), jnp.float32),
            pltpu.VMEM((quads, rows, cells, cols), jnp.float32),
            pltpu.VMEM((2, rows + 2, cells + 2 * margin, cols), jnp.float32),
            pltpu.VMEM((2, rows + 2, cells + 2 * margin, cols), jnp.float32),
        ]
        + [pltpu.SemaphoreType.DMA((2 * parts,))] * 4,
        compiler_params=pltpu.CompilerParams(
            collective_id=2 if transposed else 1, has_side_effects=True, vmem_limit_bytes=40 * 2**20
        ),
    )(coef_columns, values)


def reduction(count, part_ref, half_in, half_sum, quarter_in, quarter_sum, piece_in, full, send_sem, recv_sem, peer_send, peer_recv, back_send, back_recv):
    rows = part_ref.shape[0]
    peers = count // 4
    half, quarter, piece = rows // 2, rows // 4, rows // count
    me = lax.axis_index("row")
    low, mid, top = lax.rem(me, 2), lax.rem(me // 2, 2), me // 4
    pair = me + 1 - 2 * low
    across = me + 2 - 4 * mid

    def other(step):
        return lax.rem(top + step, peers)

    def copy_to(source, target, sends, recvs, slot, where):
        return pltpu.make_async_remote_copy(
            src_ref=source,
            dst_ref=target,
            send_sem=sends.at[slot],
            recv_sem=recvs.at[slot],
            device_id={"row": where},
            device_id_type=pl.DeviceIdType.MESH,
        )

    first = copy_to(
        part_ref.at[pl.ds(pl.multiple_of((1 - low) * half, 8), half)], half_in, send_sem, recv_sem, 0, pair
    )
    first.start()
    yield
    first.wait()
    half_sum[...] = part_ref[pl.ds(pl.multiple_of(low * half, 8), half)] + half_in[...]
    second = copy_to(
        half_sum.at[pl.ds(pl.multiple_of((1 - mid) * quarter, 8), quarter)], quarter_in, send_sem, recv_sem, 1, across
    )
    second.start()
    yield
    second.wait()
    quarter_sum[...] = half_sum[pl.ds(pl.multiple_of(mid * quarter, 8), quarter)] + quarter_in[...]
    outgoing = [
        copy_to(
            quarter_sum.at[pl.ds(pl.multiple_of(other(step) * piece, 8), piece)],
            piece_in.at[step],
            peer_send,
            peer_recv,
            step,
            other(step) * 4 + lax.rem(me, 4),
        )
        for step in range(1, peers)
    ]
    for copy in outgoing:
        copy.start()
    yield
    total = quarter_sum[pl.ds(pl.multiple_of(top * piece, 8), piece)]
    for step, copy in enumerate(outgoing, 1):
        copy.wait()
        total = total + piece_in[step]
    base = low * half + mid * quarter
    mine = pl.ds(pl.multiple_of(base + top * piece, 8), piece)
    full[mine] = total
    returning = [
        copy_to(full.at[mine], full.at[mine], back_send, back_recv, step, other(step) * 4 + lax.rem(me, 4))
        for step in range(1, peers)
    ]
    for copy in returning:
        copy.start()
    yield
    for copy in returning:
        copy.wait()
    own_quarter = full.at[pl.ds(pl.multiple_of(base, 8), quarter)]
    third = copy_to(own_quarter, own_quarter, send_sem, recv_sem, 2, across)
    third.start()
    yield
    third.wait()
    own_half = full.at[pl.ds(pl.multiple_of(low * half, 8), half)]
    fourth = copy_to(own_half, own_half, send_sem, recv_sem, 3, pair)
    fourth.start()
    yield
    fourth.wait()


def reduction_scratch(count, rows, cols):
    peers = count // 4
    return [
        pltpu.VMEM((rows // 2, cols), jnp.float32),
        pltpu.VMEM((rows // 2, cols), jnp.float32),
        pltpu.VMEM((rows // 4, cols), jnp.float32),
        pltpu.VMEM((rows // 4, cols), jnp.float32),
        pltpu.VMEM((peers, rows // count, cols), jnp.float32),
        pltpu.VMEM((rows, cols), jnp.float32),
        pltpu.SemaphoreType.DMA((4,)),
        pltpu.SemaphoreType.DMA((4,)),
    ] + [pltpu.SemaphoreType.DMA((peers,))] * 4


tile = 32


def tile_inverse(block):
    shape = (tile, tile)
    row_ids = lax.broadcasted_iota(jnp.int32, shape, 0)
    col_ids = lax.broadcasted_iota(jnp.int32, shape, 1)
    right = (row_ids == col_ids).astype(jnp.float32)
    left = block
    scale = jnp.zeros(shape, jnp.float32)
    for start in range(0, tile, 8):
        columns = [
            jnp.broadcast_to(left[start:, start + k : start + k + 1], (tile - start, tile)) for k in range(8)
        ]
        below_left, below_right = left[start:], right[start:]
        ids = row_ids[start:]
        for j in range(8):
            pivot = columns[j][j : j + 1]
            factor = jnp.where(ids > start + j, columns[j] * (1.0 / pivot), 0.0)
            scale = jnp.where(row_ids == start + j, lax.rsqrt(pivot), scale)
            for k in range(j + 1, 8):
                columns[k] = columns[k] - factor * columns[k][j : j + 1]
            below_left = below_left - factor * below_left[j : j + 1]
            below_right = below_right - factor * below_right[j : j + 1]
        if start:
            left = jnp.concatenate([left[:start], below_left], axis=0)
            right = jnp.concatenate([right[:start], below_right], axis=0)
        else:
            left, right = below_left, below_right
    return right * scale


def mul(a, b, contract):
    return lax.dot_general(a, b, ((contract[0:1], contract[1:2]), ((), ())), precision=exact, preferred_element_type=jnp.float32)


def sum_kernel(count, product_ref, gram_ref, cross_ref, gram_part, cross_part, *scratch):
    size = gram_ref.shape[0]
    side = size // 2
    gram_scratch, cross_scratch = scratch[:12], scratch[12:]
    gram_full, cross_full = gram_scratch[5], cross_scratch[5]
    me = lax.axis_index("row")
    low, mid, top = lax.rem(me, 2), lax.rem(me // 2, 2), me // 4
    peers = count // 4
    barrier = pltpu.get_barrier_semaphore()
    friends = [me + 1 - 2 * low, me + 2 - 4 * mid]
    friends += [lax.rem(top + step, peers) * 4 + lax.rem(me, 4) for step in range(1, peers)]
    for friend in friends:
        pl.semaphore_signal(barrier, inc=1, device_id={"row": friend}, device_id_type=pl.DeviceIdType.MESH)
    gram_part[:side] = product_ref[:side, :side]
    gram_part[side:size] = product_ref[side:size, :side]
    gram_part[size : size + side] = product_ref[side:size, side:]
    if gram_part.shape[0] > size + side:
        gram_part[size + side :] = jnp.zeros((gram_part.shape[0] - size - side, side), jnp.float32)
    cross_part[:size] = product_ref[size:, :side]
    cross_part[size:] = product_ref[size:, side:]
    pl.semaphore_wait(barrier, len(friends))
    gram_steps = reduction(count, gram_part, *gram_scratch)
    cross_steps = reduction(count, cross_part, *cross_scratch)
    for _ in range(7):
        next(gram_steps, None)
        next(cross_steps, None)
    gram_ref[:side, :side] = gram_full[:side]
    gram_ref[side:, :side] = gram_full[side:size]
    gram_ref[:side, side:] = gram_full[side:size].T
    gram_ref[side:, side:] = gram_full[size : size + side]
    cross_ref[:, :side] = cross_full[:size]
    cross_ref[:, side:] = cross_full[size:]


def device_sum(products):
    count = lax.axis_size("row")
    size = products.shape[1]
    side = size // 2
    unit = 8 * count
    gram_rows = (size + side + unit - 1) // unit * unit
    shape = jax.ShapeDtypeStruct((size, size), jnp.float32)
    whole = pl.BlockSpec(memory_space=pltpu.VMEM)
    return pl.pallas_call(
        functools.partial(sum_kernel, count),
        out_shape=(shape, shape),
        in_specs=[whole],
        out_specs=(whole, whole),
        scratch_shapes=[
            pltpu.VMEM((gram_rows, side), jnp.float32),
            pltpu.VMEM((2 * size, side), jnp.float32),
        ]
        + reduction_scratch(count, gram_rows, side)
        + reduction_scratch(count, 2 * size, side),
        compiler_params=pltpu.CompilerParams(collective_id=0, has_side_effects=True, vmem_limit_bytes=24 * 2**20),
    )(products)


def factor_kernel(gram_ref, cross_ref, bar_ref, inv_ref, mix_ref, work):
    size = gram_ref.shape[0]
    row_ids = lax.broadcasted_iota(jnp.int32, (size, size), 0)
    col_ids = lax.broadcasted_iota(jnp.int32, (size, size), 1)
    work[:, :size] = gram_ref[...]
    work[:, size:] = (row_ids == col_ids).astype(jnp.float32)
    for start in range(0, size, tile):
        stop = start + tile
        small = tile_inverse(work[start:stop, start:stop])
        panel = mul(small, work[start:stop, :], (1, 0))
        work[start:stop, :] = panel
        if stop < size:
            update = mul(panel[:, :size].T, panel, (1, 0))
            work[stop:, :] = work[stop:, :] - update[stop:]
    upper = jnp.where(row_ids <= col_ids, work[:, :size], 0.0)
    inverse = jnp.where(row_ids >= col_ids, work[:, size:], 0.0)
    inv_ref[...] = inverse
    bar = jnp.where(row_ids <= col_ids, bar_ref[...], 0.0)
    middle = mul(upper, bar, (1, 1)) - mul(cross_ref[...], inverse, (1, 1))
    symmetric = jnp.where(row_ids >= col_ids, middle, middle.T)
    mix_ref[...] = mul(inverse.T, mul(symmetric, inverse, (1, 0)), (1, 0))


def factor(gram, cross, r_bar):
    size = gram.shape[0]
    shape = jax.ShapeDtypeStruct((size, size), jnp.float32)
    whole = pl.BlockSpec(memory_space=pltpu.VMEM)
    return pl.pallas_call(
        factor_kernel,
        out_shape=(shape, shape),
        in_specs=[whole] * 3,
        out_specs=(whole, whole),
        scratch_shapes=[pltpu.VMEM((size, 2 * size), jnp.float32)],
        compiler_params=pltpu.CompilerParams(vmem_limit_bytes=24 * 2**20),
    )(gram, cross, r_bar)


def halves(value):
    high = value.astype(jnp.bfloat16)
    return high, (value - high.astype(jnp.float32)).astype(jnp.bfloat16)


def three(left, high, low):
    left_high, left_low = halves(left)
    dot = functools.partial(jnp.dot, preferred_element_type=jnp.float32)
    return dot(left_high, high) + (dot(left_high, low) + dot(left_low, high))


def grad_kernel(bar_ref, z_ref, noise_ref, inv_ref, mix_ref, z_out, noise_out, inv_high, inv_low, mix_high, mix_low):
    @pl.when(pl.program_id(0) == 0)
    def _():
        inv_high[...], inv_low[...] = halves(inv_ref[...])
        mix_high[...], mix_low[...] = halves(mix_ref[...])

    stacked = jnp.concatenate([z_ref[...], noise_ref[...]], axis=1)
    grad = three(bar_ref[...], inv_high[...], inv_low[...]) + three(stacked, mix_high[...], mix_low[...])
    z_out[...] = grad[:, : z_out.shape[1]]
    noise_out[...] = grad[:, z_out.shape[1] :]


def gradient(bar_rows, z_rows, noise_rows, inverse, mix):
    rows, size = bar_rows.shape
    block = rows // 8
    square = pl.BlockSpec((size, size), lambda i: (0, 0))

    def strip(value):
        return pl.BlockSpec((block, value.shape[1]), lambda i: (i, 0))

    return pl.pallas_call(
        grad_kernel,
        grid=(8,),
        out_shape=(
            jax.ShapeDtypeStruct(z_rows.shape, jnp.float32),
            jax.ShapeDtypeStruct(noise_rows.shape, jnp.float32),
        ),
        in_specs=[strip(bar_rows), strip(z_rows), strip(noise_rows), square, square],
        out_specs=(strip(z_rows), strip(noise_rows)),
        scratch_shapes=[pltpu.VMEM((size, size), jnp.bfloat16)] * 4,
        compiler_params=pltpu.CompilerParams(vmem_limit_bytes=24 * 2**20),
    )(bar_rows, z_rows, noise_rows, inverse, mix)


def on_device(cell_coeffs, z_factor, noise_cols, q_bar, r_bar):
    scaled = cell_coeffs * jnp.array(rate_scales, jnp.float32)[:, None, None]
    rank_cols = z_factor.shape[3]
    coef_columns = scaled.reshape(-1, scaled.shape[2]).T

    z_rows = second_order(coef_columns, z_factor, False).reshape(-1, rank_cols)
    noise_rows = noise_cols.reshape(-1, noise_cols.shape[3])
    flat_rows = jnp.concatenate([z_rows, noise_rows], axis=1)
    bar_rows = q_bar.reshape(-1, q_bar.shape[3])
    both = jnp.concatenate([flat_rows, bar_rows], axis=1)
    products = lax.dot_general(both, flat_rows, (((0,), (0,)), ((), ())), precision=lax.Precision.HIGH)
    gram, cross = device_sum(products)
    inverse, mix = factor(gram, cross, r_bar)
    z_part, noise_part = gradient(bar_rows, z_rows, noise_rows, inverse, mix)
    z_grad = second_order(coef_columns, z_part.reshape(z_factor.shape), True)
    return (z_grad, noise_part.reshape(noise_cols.shape))


def solution(mesh):
    return jax.shard_map(
        on_device,
        mesh=mesh,
        in_specs=(
            P(None, "row", None),
            P(None, ("grp", "row"), None, None),
            P(None, ("grp", "row"), None, None),
            P(None, ("grp", "row"), None, None),
            P("grp", None),
        ),
        out_specs=(P(None, ("grp", "row"), None, None), P(None, ("grp", "row"), None, None)),
        check_vma=False,
    )
```

```python
import functools

import jax
import jax.numpy as jnp
from jax import lax
from jax.experimental import pallas as pl
from jax.experimental.pallas import tpu as pltpu
from jax.sharding import PartitionSpec as P

rate_scales = (0.4, 0.4, 0.1, 0.2, 0.1, 0.1)
exact = lax.Precision.HIGHEST


parts = 4
margin = 8


def step_kernel(count, transposed, coef_ref, value_ref, out_ref, coefs, first, source, source_two, send_low, recv_low, send_high, recv_high):
    rows, cells, cols = value_ref.shape[1:]
    chunk = cells // parts
    me = lax.axis_index("row")
    has_low, has_high = me > 0, me < count - 1

    def link(buffer, stage, piece, upward):
        cut = pl.ds(margin + piece * chunk, chunk)
        sends, recvs = (send_high, recv_high) if upward else (send_low, recv_low)
        slot = stage * parts + piece
        return pltpu.make_async_remote_copy(
            src_ref=buffer.at[:, rows if upward else 1, cut],
            dst_ref=buffer.at[:, 0 if upward else rows + 1, cut],
            send_sem=sends.at[slot],
            recv_sem=recvs.at[slot],
            device_id={"row": me + 1 if upward else me - 1},
            device_id_type=pl.DeviceIdType.MESH,
        )

    def send(buffer, stage, piece):
        @pl.when(has_high)
        def _():
            link(buffer, stage, piece, True).start()

        @pl.when(has_low)
        def _():
            link(buffer, stage, piece, False).start()

    def receive(buffer, stage, piece):
        @pl.when(has_low)
        def _():
            link(buffer, stage, piece, True).wait_recv()

        @pl.when(has_high)
        def _():
            link(buffer, stage, piece, False).wait_recv()

    barrier = pltpu.get_barrier_semaphore()

    @pl.when(has_low)
    def _():
        pl.semaphore_signal(barrier, inc=1, device_id={"row": me - 1}, device_id_type=pl.DeviceIdType.MESH)

    @pl.when(has_high)
    def _():
        pl.semaphore_signal(barrier, inc=1, device_id={"row": me + 1}, device_id_type=pl.DeviceIdType.MESH)

    def coef(kind, row, piece):
        return coefs[kind * rows + row, piece * chunk : (piece + 1) * chunk]

    def at(piece):
        return slice(piece * chunk, (piece + 1) * chunk)

    def inner(piece, shift=0):
        return slice(margin + piece * chunk + shift, margin + (piece + 1) * chunk + shift)

    def spread(kind):
        for row in range(rows):
            index = kind * rows + row
            coefs[index] = jnp.broadcast_to(coef_ref[:, index : index + 1], (cells, cols))

    def fill(buffer, values, piece):
        for row in range(rows):
            for quad in range(2):
                value = values[quad, row, at(piece)]
                if transposed:
                    value = value * coef(5, row, piece)
                buffer[quad, row + 1, inner(piece)] = value

    def zero_rim(buffer):
        for quad in range(2):
            for row in range(rows):
                buffer[quad, row + 1, :margin] = jnp.zeros((margin, cols), jnp.float32)
                buffer[quad, row + 1, margin + cells :] = jnp.zeros((margin, cols), jnp.float32)

        @pl.when(jnp.logical_not(has_low))
        def _():
            buffer[:, 0] = jnp.zeros(buffer.shape[:1] + buffer.shape[2:], jnp.float32)

        @pl.when(jnp.logical_not(has_high))
        def _():
            buffer[:, rows + 1] = jnp.zeros(buffer.shape[:1] + buffer.shape[2:], jnp.float32)

    def local(values, buffer, row, piece):
        xa, pa, xb, pb = [values[quad, row, at(piece)] for quad in range(4)]
        detuning, mech, coupling, cavity, phonon, hopping = [coef(kind, row, piece) for kind in range(6)]
        sums = []
        for quad in range(2):
            total = buffer[quad, row + 1, inner(piece, -1)] + buffer[quad, row + 1, inner(piece, 1)]
            if row > 0:
                total = total + buffer[quad, row, inner(piece)]
            if row < rows - 1:
                total = total + buffer[quad, row + 2, inner(piece)]
            sums.append(total)
        if transposed:
            return (
                -0.5 * cavity * xa + detuning * pa - 2.0 * coupling * pb + sums[1],
                -detuning * xa - 0.5 * cavity * pa - sums[0],
                -2.0 * coupling * pa - mech * pb,
                mech * xb - 0.5 * phonon * pb,
            )
        return (
            -0.5 * cavity * xa - detuning * pa - hopping * sums[1],
            detuning * xa - 0.5 * cavity * pa - 2.0 * coupling * xb + hopping * sums[0],
            mech * pb,
            -mech * xb - 0.5 * phonon * pb - 2.0 * coupling * xa,
        )

    def edges(buffer, piece):
        found = []
        for row, halo in ((0, 0), (rows - 1, rows + 1)):
            light_x, light_p = buffer[0, halo, inner(piece)], buffer[1, halo, inner(piece)]
            if transposed:
                found.append((row, light_p, -light_x))
            else:
                hopping = coef(5, row, piece)
                found.append((row, -hopping * light_p, hopping * light_x))
        return found

    spread(5)
    fill(source, value_ref, 0)

    pl.semaphore_wait(barrier, jnp.where(me > 0, 1, 0) + jnp.where(me < count - 1, 1, 0))

    send(source, 0, 0)
    for piece in range(1, parts):
        fill(source, value_ref, piece)
        send(source, 0, piece)
    zero_rim(source)
    zero_rim(source_two)
    for kind in range(5):
        spread(kind)
    for piece in range(parts):
        for row in range(rows):
            for quad, value in enumerate(local(value_ref, source, row, piece)):
                first[quad, row, at(piece)] = value
    for piece in range(parts):
        receive(source, 0, piece)
        for row, add_x, add_p in edges(source, piece):
            first[0, row, at(piece)] = first[0, row, at(piece)] + add_x
            first[1, row, at(piece)] = first[1, row, at(piece)] + add_p
        fill(source_two, first, piece)
        send(source_two, 1, piece)
    for piece in range(parts):
        for row in range(rows):
            for quad, value in enumerate(local(first, source_two, row, piece)):
                out_ref[quad, row, at(piece)] = (
                    value_ref[quad, row, at(piece)] + first[quad, row, at(piece)] + 0.5 * value
                )
    for piece in range(parts):
        receive(source_two, 1, piece)
        for row, add_x, add_p in edges(source_two, piece):
            out_ref[0, row, at(piece)] = out_ref[0, row, at(piece)] + 0.5 * add_x
            out_ref[1, row, at(piece)] = out_ref[1, row, at(piece)] + 0.5 * add_p
    for stage, buffer in enumerate((source, source_two)):
        for piece in range(parts):

            @pl.when(has_high)
            def _():
                link(buffer, stage, piece, True).wait_send()

            @pl.when(has_low)
            def _():
                link(buffer, stage, piece, False).wait_send()


def second_order(coef_columns, values, transposed):
    count = lax.axis_size("row")
    quads, rows, cells, cols = values.shape
    whole = pl.BlockSpec(memory_space=pltpu.VMEM)
    return pl.pallas_call(
        functools.partial(step_kernel, count, transposed),
        out_shape=jax.ShapeDtypeStruct(values.shape, jnp.float32),
        in_specs=[whole] * 2,
        out_specs=whole,
        scratch_shapes=[
            pltpu.VMEM((coef_columns.shape[1], cells, cols), jnp.float32),
            pltpu.VMEM((quads, rows, cells, cols), jnp.float32),
            pltpu.VMEM((2, rows + 2, cells + 2 * margin, cols), jnp.float32),
            pltpu.VMEM((2, rows + 2, cells + 2 * margin, cols), jnp.float32),
        ]
        + [pltpu.SemaphoreType.DMA((2 * parts,))] * 4,
        compiler_params=pltpu.CompilerParams(
            collective_id=2 if transposed else 1, has_side_effects=True, vmem_limit_bytes=40 * 2**20
        ),
    )(coef_columns, values)


def reduction(count, part_ref, half_in, half_sum, quarter_in, quarter_sum, piece_in, full, send_sem, recv_sem, peer_send, peer_recv, back_send, back_recv):
    rows = part_ref.shape[0]
    peers = count // 4
    half, quarter, piece = rows // 2, rows // 4, rows // count
    me = lax.axis_index("row")
    low, mid, top = lax.rem(me, 2), lax.rem(me // 2, 2), me // 4
    pair = me + 1 - 2 * low
    across = me + 2 - 4 * mid

    def other(step):
        return lax.rem(top + step, peers)

    def copy_to(source, target, sends, recvs, slot, where):
        return pltpu.make_async_remote_copy(
            src_ref=source,
            dst_ref=target,
            send_sem=sends.at[slot],
            recv_sem=recvs.at[slot],
            device_id={"row": where},
            device_id_type=pl.DeviceIdType.MESH,
        )

    first = copy_to(
        part_ref.at[pl.ds(pl.multiple_of((1 - low) * half, 8), half)], half_in, send_sem, recv_sem, 0, pair
    )
    first.start()
    yield
    first.wait()
    half_sum[...] = part_ref[pl.ds(pl.multiple_of(low * half, 8), half)] + half_in[...]
    second = copy_to(
        half_sum.at[pl.ds(pl.multiple_of((1 - mid) * quarter, 8), quarter)], quarter_in, send_sem, recv_sem, 1, across
    )
    second.start()
    yield
    second.wait()
    quarter_sum[...] = half_sum[pl.ds(pl.multiple_of(mid * quarter, 8), quarter)] + quarter_in[...]
    outgoing = [
        copy_to(
            quarter_sum.at[pl.ds(pl.multiple_of(other(step) * piece, 8), piece)],
            piece_in.at[step],
            peer_send,
            peer_recv,
            step,
            other(step) * 4 + lax.rem(me, 4),
        )
        for step in range(1, peers)
    ]
    for copy in outgoing:
        copy.start()
    yield
    total = quarter_sum[pl.ds(pl.multiple_of(top * piece, 8), piece)]
    for step, copy in enumerate(outgoing, 1):
        copy.wait()
        total = total + piece_in[step]
    base = low * half + mid * quarter
    mine = pl.ds(pl.multiple_of(base + top * piece, 8), piece)
    full[mine] = total
    returning = [
        copy_to(full.at[mine], full.at[mine], back_send, back_recv, step, other(step) * 4 + lax.rem(me, 4))
        for step in range(1, peers)
    ]
    for copy in returning:
        copy.start()
    yield
    for copy in returning:
        copy.wait()
    own_quarter = full.at[pl.ds(pl.multiple_of(base, 8), quarter)]
    third = copy_to(own_quarter, own_quarter, send_sem, recv_sem, 2, across)
    third.start()
    yield
    third.wait()
    own_half = full.at[pl.ds(pl.multiple_of(low * half, 8), half)]
    fourth = copy_to(own_half, own_half, send_sem, recv_sem, 3, pair)
    fourth.start()
    yield
    fourth.wait()


def reduction_scratch(count, rows, cols):
    peers = count // 4
    return [
        pltpu.VMEM((rows // 2, cols), jnp.float32),
        pltpu.VMEM((rows // 2, cols), jnp.float32),
        pltpu.VMEM((rows // 4, cols), jnp.float32),
        pltpu.VMEM((rows // 4, cols), jnp.float32),
        pltpu.VMEM((peers, rows // count, cols), jnp.float32),
        pltpu.VMEM((rows, cols), jnp.float32),
        pltpu.SemaphoreType.DMA((4,)),
        pltpu.SemaphoreType.DMA((4,)),
    ] + [pltpu.SemaphoreType.DMA((peers,))] * 4


tile = 32


def tile_inverse(block):
    shape = (tile, tile)
    row_ids = lax.broadcasted_iota(jnp.int32, shape, 0)
    col_ids = lax.broadcasted_iota(jnp.int32, shape, 1)
    right = (row_ids == col_ids).astype(jnp.float32)
    left = block
    scale = jnp.zeros(shape, jnp.float32)
    for start in range(0, tile, 8):
        columns = [
            jnp.broadcast_to(left[start:, start + k : start + k + 1], (tile - start, tile)) for k in range(8)
        ]
        below_left, below_right = left[start:], right[start:]
        ids = row_ids[start:]
        for j in range(8):
            pivot = columns[j][j : j + 1]
            factor = jnp.where(ids > start + j, columns[j] * (1.0 / pivot), 0.0)
            scale = jnp.where(row_ids == start + j, lax.rsqrt(pivot), scale)
            for k in range(j + 1, 8):
                columns[k] = columns[k] - factor * columns[k][j : j + 1]
            below_left = below_left - factor * below_left[j : j + 1]
            below_right = below_right - factor * below_right[j : j + 1]
        if start:
            left = jnp.concatenate([left[:start], below_left], axis=0)
            right = jnp.concatenate([right[:start], below_right], axis=0)
        else:
            left, right = below_left, below_right
    return right * scale


def mul(a, b, contract):
    return lax.dot_general(a, b, ((contract[0:1], contract[1:2]), ((), ())), precision=exact, preferred_element_type=jnp.float32)


def sum_kernel(count, product_ref, gram_ref, cross_ref, gram_part, cross_part, *scratch):
    size = gram_ref.shape[0]
    side = size // 2
    gram_scratch, cross_scratch = scratch[:12], scratch[12:]
    gram_full, cross_full = gram_scratch[5], cross_scratch[5]
    me = lax.axis_index("row")
    low, mid, top = lax.rem(me, 2), lax.rem(me // 2, 2), me // 4
    peers = count // 4
    barrier = pltpu.get_barrier_semaphore()
    friends = [me + 1 - 2 * low, me + 2 - 4 * mid]
    friends += [lax.rem(top + step, peers) * 4 + lax.rem(me, 4) for step in range(1, peers)]
    for friend in friends:
        pl.semaphore_signal(barrier, inc=1, device_id={"row": friend}, device_id_type=pl.DeviceIdType.MESH)
    gram_part[:side] = product_ref[:side, :side]
    gram_part[side:size] = product_ref[side:size, :side]
    gram_part[size : size + side] = product_ref[side:size, side:]
    if gram_part.shape[0] > size + side:
        gram_part[size + side :] = jnp.zeros((gram_part.shape[0] - size - side, side), jnp.float32)
    cross_part[:size] = product_ref[size:, :side]
    cross_part[size:] = product_ref[size:, side:]
    pl.semaphore_wait(barrier, len(friends))
    gram_steps = reduction(count, gram_part, *gram_scratch)
    cross_steps = reduction(count, cross_part, *cross_scratch)
    for _ in range(7):
        next(gram_steps, None)
        next(cross_steps, None)
    gram_ref[:side, :side] = gram_full[:side]
    gram_ref[side:, :side] = gram_full[side:size]
    gram_ref[:side, side:] = gram_full[side:size].T
    gram_ref[side:, side:] = gram_full[size : size + side]
    cross_ref[:, :side] = cross_full[:size]
    cross_ref[:, side:] = cross_full[size:]


def device_sum(products):
    count = lax.axis_size("row")
    size = products.shape[1]
    side = size // 2
    unit = 8 * count
    gram_rows = (size + side + unit - 1) // unit * unit
    shape = jax.ShapeDtypeStruct((size, size), jnp.float32)
    whole = pl.BlockSpec(memory_space=pltpu.VMEM)
    return pl.pallas_call(
        functools.partial(sum_kernel, count),
        out_shape=(shape, shape),
        in_specs=[whole],
        out_specs=(whole, whole),
        scratch_shapes=[
            pltpu.VMEM((gram_rows, side), jnp.float32),
            pltpu.VMEM((2 * size, side), jnp.float32),
        ]
        + reduction_scratch(count, gram_rows, side)
        + reduction_scratch(count, 2 * size, side),
        compiler_params=pltpu.CompilerParams(collective_id=0, has_side_effects=True, vmem_limit_bytes=24 * 2**20),
    )(products)


def factor_kernel(gram_ref, cross_ref, bar_ref, inv_ref, mix_ref, work):
    size = gram_ref.shape[0]
    row_ids = lax.broadcasted_iota(jnp.int32, (size, size), 0)
    col_ids = lax.broadcasted_iota(jnp.int32, (size, size), 1)
    work[:, :size] = gram_ref[...]
    work[:, size:] = (row_ids == col_ids).astype(jnp.float32)
    for start in range(0, size, tile):
        stop = start + tile
        small = tile_inverse(work[start:stop, start:stop])
        panel = mul(small, work[start:stop, :], (1, 0))
        work[start:stop, :] = panel
        if stop < size:
            base, end = stop // 128 * 128, size + (stop + 127) // 128 * 128
            update = mul(panel[:, base:size].T, panel[:, base:end], (1, 0))
            work[stop:, base:end] = work[stop:, base:end] - update[stop - base :]
    upper = jnp.where(row_ids <= col_ids, work[:, :size], 0.0)
    inverse = jnp.where(row_ids >= col_ids, work[:, size:], 0.0)
    inv_ref[...] = inverse
    bar = jnp.where(row_ids <= col_ids, bar_ref[...], 0.0)
    middle = mul(upper, bar, (1, 1)) - mul(cross_ref[...], inverse, (1, 1))
    symmetric = jnp.where(row_ids >= col_ids, middle, middle.T)
    mix_ref[...] = mul(inverse.T, mul(symmetric, inverse, (1, 0)), (1, 0))


def factor(gram, cross, r_bar):
    size = gram.shape[0]
    shape = jax.ShapeDtypeStruct((size, size), jnp.float32)
    whole = pl.BlockSpec(memory_space=pltpu.VMEM)
    return pl.pallas_call(
        factor_kernel,
        out_shape=(shape, shape),
        in_specs=[whole] * 3,
        out_specs=(whole, whole),
        scratch_shapes=[pltpu.VMEM((size, 2 * size), jnp.float32)],
        compiler_params=pltpu.CompilerParams(vmem_limit_bytes=24 * 2**20),
    )(gram, cross, r_bar)


def halves(value):
    high = value.astype(jnp.bfloat16)
    return high, (value - high.astype(jnp.float32)).astype(jnp.bfloat16)


def three(left, high, low):
    left_high, left_low = halves(left)
    dot = functools.partial(jnp.dot, preferred_element_type=jnp.float32)
    return dot(left_high, high) + (dot(left_high, low) + dot(left_low, high))


def grad_kernel(bar_ref, z_ref, noise_ref, inv_ref, mix_ref, z_out, noise_out, inv_high, inv_low, mix_high, mix_low):
    @pl.when(pl.program_id(0) == 0)
    def _():
        inv_high[...], inv_low[...] = halves(inv_ref[...])
        mix_high[...], mix_low[...] = halves(mix_ref[...])

    stacked = jnp.concatenate([z_ref[...], noise_ref[...]], axis=1)
    grad = three(bar_ref[...], inv_high[...], inv_low[...]) + three(stacked, mix_high[...], mix_low[...])
    z_out[...] = grad[:, : z_out.shape[1]]
    noise_out[...] = grad[:, z_out.shape[1] :]


def gradient(bar_rows, z_rows, noise_rows, inverse, mix):
    rows, size = bar_rows.shape
    block = rows // 8
    square = pl.BlockSpec((size, size), lambda i: (0, 0))

    def strip(value):
        return pl.BlockSpec((block, value.shape[1]), lambda i: (i, 0))

    return pl.pallas_call(
        grad_kernel,
        grid=(8,),
        out_shape=(
            jax.ShapeDtypeStruct(z_rows.shape, jnp.float32),
            jax.ShapeDtypeStruct(noise_rows.shape, jnp.float32),
        ),
        in_specs=[strip(bar_rows), strip(z_rows), strip(noise_rows), square, square],
        out_specs=(strip(z_rows), strip(noise_rows)),
        scratch_shapes=[pltpu.VMEM((size, size), jnp.bfloat16)] * 4,
        compiler_params=pltpu.CompilerParams(vmem_limit_bytes=24 * 2**20),
    )(bar_rows, z_rows, noise_rows, inverse, mix)


def on_device(cell_coeffs, z_factor, noise_cols, q_bar, r_bar):
    scaled = cell_coeffs * jnp.array(rate_scales, jnp.float32)[:, None, None]
    rank_cols = z_factor.shape[3]
    coef_columns = scaled.reshape(-1, scaled.shape[2]).T

    z_rows = second_order(coef_columns, z_factor, False).reshape(-1, rank_cols)
    noise_rows = noise_cols.reshape(-1, noise_cols.shape[3])
    flat_rows = jnp.concatenate([z_rows, noise_rows], axis=1)
    bar_rows = q_bar.reshape(-1, q_bar.shape[3])
    both = jnp.concatenate([flat_rows, bar_rows], axis=1)
    products = lax.dot_general(both, flat_rows, (((0,), (0,)), ((), ())), precision=lax.Precision.HIGH)
    gram, cross = device_sum(products)
    inverse, mix = factor(gram, cross, r_bar)
    z_part, noise_part = gradient(bar_rows, z_rows, noise_rows, inverse, mix)
    z_grad = second_order(coef_columns, z_part.reshape(z_factor.shape), True)
    return (z_grad, noise_part.reshape(noise_cols.shape))


def solution(mesh):
    return jax.shard_map(
        on_device,
        mesh=mesh,
        in_specs=(
            P(None, "row", None),
            P(None, ("grp", "row"), None, None),
            P(None, ("grp", "row"), None, None),
            P(None, ("grp", "row"), None, None),
            P("grp", None),
        ),
        out_specs=(P(None, ("grp", "row"), None, None), P(None, ("grp", "row"), None, None)),
        check_vma=False,
    )
```
